256 devices in a mesh: dp: 4 (over z_hi), passage: 64 (over z_lo, x, y, core).
Axes of the slice: x: 4, y: 4, z: 8 (z_hi: 4, z_lo: 2; z = z_hi * 2 + z_lo), core: 2. Of those that a mesh axis runs over, the one named last changes fastest.
Arguments:
- question: bfloat16 [8, 32, 4096], P('dp', None, 'passage'), may hold values from -6 to 6
- norm_gain: bfloat16 [4096], P('passage'), may hold values from 0.5 to 1.5
- w_qkv: bfloat16 [4096, 6144], P('passage'), may hold values from -0.09375 to 0.09375
- mem_keys: bfloat16 [128, 8, 200, 2048], P('passage', 'dp'), may hold values from -122 to 122
- mem_values: bfloat16 [128, 8, 200, 2048], P('passage', 'dp'), may hold values from -6 to 6
- mem_length: int32 [128, 8], P('passage', 'dp'), may hold values from 2 to 200
- owner: int32 [128, 4, 2], P('passage', 'dp'), may hold values from 0 to 1, each once within a row
- d_context: bfloat16 [128, 8, 32, 2048], P('passage', 'dp'), may hold values from -0.29882812 to 0.29882812
Outputs:
- context: bfloat16 [128, 8, 32, 2048], P('passage', 'dp')
- d_question: bfloat16 [8, 32, 4096], P('dp', None, 'passage')
- d_gain: float32 [4096], P('passage')
- d_weight: float32 [4096, 6144], P('passage')
The draws below stay inside these ranges and needn't reach their ends.
Inputs may be any that keep to these rules, and one draw needn't show every extreme that they name: `owner`: the 2 slots of each passage index and group hold one passage of each of the group's questions.
All inputs are finite; a program needn't handle non-finite values.
Results may differ from the reference program's by a relative error of at most 0.015.
The reference program's roundings to bfloat16 on the way (of `scaled`, `qkv`, `prob_b`, `d_scores` and `d_pre`) count: a program that leaves them out, or rounds other values in their place, can miss the bound.
Values may be sent and summed in bfloat16 or wider, within the bound.
No kernel may reach another device: no remote copies, remote signals or barrier semaphores. Data moves between devices by JAX's collectives and lax.ppermute only.
A program may use at most 128 MiB of HBM per device.

```python
import math
import jax
import jax.numpy as jnp
from jax import lax

D = 4096
HEADS = 32
QLEN = 32
MEMLEN = 200
QUEST_DEV = 2
INNER = 2048
QUESTIONS = 8
PASSAGES = 128
N_DP = 4


def draw_mem_keys(key, part):
    key = jax.random.fold_in(key, 7)
    first = jax.random.fold_in(key, 0)
    shape = (PASSAGES, QUESTIONS, MEMLEN, INNER)
    result = jnp.clip(jax.random.normal(first, shape, jnp.float32), -6.0, 6.0)
    return result.astype(jnp.bfloat16)


def draw_mem_length(key, part):
    key = jax.random.fold_in(key, 5)
    drawn = jax.random.randint(key, (PASSAGES, QUESTIONS), 2, MEMLEN + 1)
    filled = (jnp.arange(PASSAGES)[:, None] + jnp.arange(QUESTIONS)[None, :]) % 3 == 0
    return jnp.where(filled, MEMLEN, drawn).astype(jnp.int32)


def steps_of(stream_key, extent, cuts, least, top_value):
    loudness = 1.0
    for dim, parts in cuts:
        steps = jax.random.uniform(jax.random.fold_in(jax.random.fold_in(stream_key, 6), dim), (parts,), jnp.float32, least / len(cuts), top_value / len(cuts))
        loudness = loudness * jnp.repeat(jnp.exp(steps), extent[dim] // parts).reshape((-1,) + (1,) * (len(extent) - 1 - dim))
    return loudness


def centred(key, shape, deviation, bound, cuts=(), held_as=jnp.bfloat16):
    values = deviation * jax.random.normal(key, shape, jnp.float32)
    if cuts:
        values = values * steps_of(key, shape, cuts, -0.22, 0.18)
    return jnp.clip(values, -bound, bound).astype(held_as)


def setup_inputs(seed: int = 0) -> dict:
    key_of = jax.random.split(jax.random.key(seed), 9)
    return {
        "question": centred(key_of[0], (QUESTIONS, QLEN, D), 1.0, 6.0, ((0, 4), (2, 64))),
        "norm_gain": jnp.clip(1.0 + 0.1 * jax.random.normal(key_of[1], (D,), jnp.float32), 0.5, 1.5).astype(jnp.bfloat16),
        "w_qkv": centred(key_of[2], (D, 3 * INNER), D ** -0.5, 0.09375, ((0, 64),)),
        "mem_keys": draw_mem_keys(jax.random.fold_in(key_of[8], 71), 0),
        "mem_values": centred(key_of[4], (PASSAGES, QUESTIONS, MEMLEN, INNER), 1.0, 6.0, ((0, 64), (1, 4))),
        "mem_length": draw_mem_length(jax.random.fold_in(key_of[8], 71), 0),
        "owner": jax.vmap(lambda own: jax.random.permutation(own, QUEST_DEV))(jax.random.split(key_of[6], PASSAGES * N_DP)).reshape((PASSAGES, N_DP, QUEST_DEV)).astype(jnp.int32),
        "d_context": centred(key_of[7], (PASSAGES, QUESTIONS, QLEN, INNER), 0.05, 0.29882812, ((0, 64), (1, 4))),
    }


EPS = 1e-06

def attend(query_rows, key_rows, value_rows, keys_mem, values_mem, length, d_out_rows):
    slots, qlen, inner = query_rows.shape
    head_dim = inner // HEADS
    scale = 1.0 / math.sqrt(head_dim)
    total = qlen + keys_mem.shape[1]
    keys = jnp.concatenate([key_rows, keys_mem], axis=1).astype(jnp.float32).reshape(slots, total, HEADS, head_dim)
    values = jnp.concatenate([value_rows, values_mem], axis=1).astype(jnp.float32).reshape(slots, total, HEADS, head_dim)
    query = query_rows.astype(jnp.float32).reshape(slots, qlen, HEADS, head_dim)
    scores = jnp.einsum('sqhd,skhd->shqk', query, keys) * scale
    position = jnp.arange(total, dtype=jnp.int32)
    live = (position[None, :] < (length.astype(jnp.int32) + qlen)[:, None])[:, None, None, :]
    masked = jnp.where(live, scores, -1e+30)
    top = lax.optimization_barrier(jnp.max(masked, axis=-1, keepdims=True))
    expo = jnp.where(live, jnp.exp(masked - top), 0.0)
    prob = expo / lax.optimization_barrier(jnp.sum(expo, axis=-1, keepdims=True))
    prob_b = prob.astype(jnp.bfloat16).astype(jnp.float32)
    context = jnp.einsum('shqk,skhd->sqhd', prob_b, values).reshape(slots, qlen, inner).astype(jnp.bfloat16)
    d_out = d_out_rows.astype(jnp.float32).reshape(slots, qlen, HEADS, head_dim)
    d_prob = jnp.einsum('sqhd,skhd->shqk', d_out, values)
    inner_sum = lax.optimization_barrier(jnp.sum(d_prob * prob, axis=-1, keepdims=True))
    d_scores = (prob * (d_prob - inner_sum) * scale).astype(jnp.bfloat16).astype(jnp.float32)
    d_query = jnp.einsum('shqk,skhd->sqhd', d_scores, keys).reshape(slots, qlen, inner)
    d_key = jnp.einsum('shqk,sqhd->skhd', d_scores[..., :qlen], query).reshape(slots, qlen, inner)
    d_value = jnp.einsum('shqk,sqhd->skhd', prob_b[..., :qlen], d_out).reshape(slots, qlen, inner)
    return (context, jnp.concatenate([d_query, d_key, d_value], axis=-1))

def reference(question, norm_gain, w_qkv, mem_keys, mem_values, mem_length, owner, d_context):
    inputs = question.astype(jnp.float32)
    rate = lax.rsqrt(lax.optimization_barrier(jnp.mean(inputs * inputs, axis=-1)) + EPS)
    gain = norm_gain.astype(jnp.float32)
    scaled = (inputs * gain).astype(jnp.bfloat16)
    pre = jnp.dot(scaled.reshape(QUESTIONS * QLEN, D), w_qkv, preferred_element_type=jnp.float32)
    pre = pre.reshape(QUESTIONS, QLEN, 3 * INNER)
    qkv = (pre * rate[..., None]).astype(jnp.bfloat16)
    groups = jnp.arange(QUESTIONS, dtype=jnp.int32) // QUEST_DEV
    which = groups[None, :] * QUEST_DEV + owner.reshape(PASSAGES, QUESTIONS).astype(jnp.int32)

    def per_passage(grad, pieces):
        own, keys_p, values_p, length_p, d_p = pieces
        rows = jnp.take(qkv, own, axis=0)
        context, slot_grad = attend(rows[..., :INNER], rows[..., INNER:2 * INNER], rows[..., 2 * INNER:], keys_p, values_p, length_p, d_p)
        return (grad.at[own].add(slot_grad), context)
    start = jnp.zeros((QUESTIONS, QLEN, 3 * INNER), jnp.float32)
    grad, context = lax.scan(per_passage, start, (which, mem_keys, mem_values, mem_length, d_context))
    d_pre = (grad * rate[..., None]).astype(jnp.bfloat16)
    d_rate = lax.optimization_barrier(jnp.sum(grad * pre, axis=-1))
    rows_scaled = scaled.reshape(QUESTIONS * QLEN, D)
    rows_pre = d_pre.reshape(QUESTIONS * QLEN, 3 * INNER)
    d_weight = jnp.dot(rows_scaled.T, rows_pre, preferred_element_type=jnp.float32)
    d_input = jnp.dot(rows_pre, w_qkv.T, preferred_element_type=jnp.float32).reshape(QUESTIONS, QLEN, D)
    d_gain = lax.optimization_barrier(jnp.sum(inputs * d_input, axis=(0, 1)))
    d_question = (gain * d_input - (d_rate * rate ** 3)[..., None] * inputs / D).astype(jnp.bfloat16)
    return (context, d_question, d_gain, d_weight)
```

```python
import functools

import jax
import jax.numpy as jnp
from jax import lax
from jax.experimental import pallas as pl
from jax.experimental.pallas import tpu as pltpu
from jax.sharding import PartitionSpec as P

D = 4096
EPS = 1e-06
QLEN = 32
ROWS = 64
FEATS = 64
MEM = 200
HALF = 1024
COLS = 3 * HALF
CHIPS = 32
COL_BLOCKS = 8
CHUNK = 48
K_AT, V_AT, PACKED = 32, 240, 448
FOLD = 0.125

BF16 = jnp.bfloat16
F32 = jnp.float32
VMEM = pl.BlockSpec(memory_space=pltpu.VMEM)
SMEM = pl.BlockSpec(memory_space=pltpu.SMEM)
PARAMS = pltpu.CompilerParams(vmem_limit_bytes=24 * 1024 * 1024)

NT = (((1,), (1,)), ((), ()))
TN = (((0,), (0,)), ((), ()))


def dot(a, b, dims=(((1,), (0,)), ((), ()))):
    return lax.dot_general(a, b, dims, preferred_element_type=F32)


def lanes_of(index, width):
    return pl.ds(pl.multiple_of(index * width, width), width)


def pack_w(core, w_ref, q_ref, gain_ref, out_ref):
    other = 1 - core[0]
    for b in range(3):
        out_ref[0:FEATS, b * HALF : (b + 1) * HALF] = w_ref[:, lanes_of(2 * b + other, HALF)]
    for j in range(4):
        out_ref[64:80, j * 128 : j * 128 + 64] = q_ref[j * 16 : (j + 1) * 16, :]
    out_ref[64:80, 512:576] = jnp.broadcast_to(gain_ref[...], (16, FEATS))


def pack_memory(core, keys_ref, values_ref, d_ref, out_ref):
    out_ref[0, 0:QLEN] = d_ref[0, 0]
    out_ref[0, K_AT : K_AT + MEM] = keys_ref[0, 0]
    out_ref[0, V_AT : V_AT + MEM] = values_ref[0, 0]


def project(core, w_ref, q_ref, gain_ref, recv_ref, part_ref, wc_ref, pair_ref, gains_ref):
    theirs = jnp.concatenate(
        [recv_ref[64:80, j * 128 : j * 128 + 64].astype(F32) for j in range(4)], axis=0
    )
    pair = jnp.concatenate([q_ref[...].astype(F32), theirs], axis=1)
    gains = jnp.concatenate(
        [gain_ref[...].astype(F32), recv_ref[64:80, 512:576].astype(F32)[0:1]], axis=1
    )
    pair_ref[...] = pair.astype(BF16)
    gains_ref[...] = gains
    scaled = (pair * gains).astype(BF16)
    for b in range(3):
        wc_ref[0:FEATS, b * HALF : (b + 1) * HALF] = w_ref[:, lanes_of(2 * b + core[0], HALF)]
    wc_ref[FEATS:, :] = recv_ref[0:FEATS, :]
    for cb in range(COL_BLOCKS):
        pre = dot(scaled, wc_ref[:, cb * 384 : (cb + 1) * 384])
        for rb in range(4):
            for t in range(3):
                part_ref[rb * COL_BLOCKS + cb, t * 16 : (t + 1) * 16, :] = pre[
                    rb * 16 : (rb + 1) * 16, t * 128 : (t + 1) * 128
                ]
    squares = jnp.sum(pair * pair, axis=1, keepdims=True)
    low = lax.broadcasted_iota(jnp.int32, (8, 128), 1) < 64
    for rb in range(4):
        tile = jnp.where(
            low, squares[rb * 16 : rb * 16 + 8], squares[rb * 16 + 8 : rb * 16 + 16]
        )
        for cb in range(COL_BLOCKS):
            part_ref[rb * COL_BLOCKS + cb, CHUNK : CHUNK + 8, :] = tile


def normalise(part_ref, qkv_ref, pre_ref, rate_ref):
    total = jnp.sum(part_ref[...], axis=0)
    rates = lax.rsqrt(total[CHUNK:] / D + EPS)
    rate = jnp.concatenate([rates[:, 0:1], rates[:, 64:65]], axis=0)
    rate = jnp.broadcast_to(rate, (16, 128))
    pre = total[:CHUNK]
    pre_ref[...] = pre
    rate_ref[...] = rate
    qkv = (pre * jnp.concatenate([rate] * 3, axis=0)).astype(BF16)
    for k in range(CHIPS):
        qkv_ref[k] = qkv


def attend(
    own, oth, qkv_ref, keys_ref, values_ref, d_ref, packed_ref, ctx_own, ctx_oth, grad_ref,
    rows, mask_q, mask_d, kcat, vcat,
):
    step = pl.program_id(0)

    @pl.when(step == 0)
    def _():
        for k in range(CHIPS):
            rb, cb = divmod(k, COL_BLOCKS)
            for t in range(3):
                at = (cb * 3 + t) * 128
                rows[rb * 16 : (rb + 1) * 16, at : at + 128] = qkv_ref[k, t * 16 : (t + 1) * 16, :]
        grad_ref[...] = jnp.zeros_like(grad_ref)
        head = lax.broadcasted_iota(jnp.int32, (128, 256), 0) // QLEN
        lane = lax.broadcasted_iota(jnp.int32, (128, 256), 1) // 64
        same = jnp.where(head == lane, 1.0, 0.0)
        mask_d[...] = same.astype(BF16)
        mask_q[...] = (same * FOLD).astype(BF16)
        for unit in range(8):
            kcat[unit, 224:256] = jnp.zeros((32, 256), BF16)
            vcat[unit, 224:256] = jnp.zeros((32, 256), BF16)

    key_at = lax.broadcasted_iota(jnp.int32, (1, 256), 1)
    lane_head = lax.broadcasted_iota(jnp.int32, (QLEN, 256), 1) // 64

    def diagonal(full):
        out = full[0:QLEN]
        for h in range(1, 4):
            out = jnp.where(lane_head == h, full[h * QLEN : (h + 1) * QLEN], out)
        return out

    for side, info in enumerate((own, oth)):
        live = key_at < info[step] + QLEN
        question = info[4 + step]
        at = pl.ds(pl.multiple_of(question * QLEN, QLEN), QLEN)
        for hg in range(4):
            unit = side * 4 + hg
            lanes = slice(hg * 256, (hg + 1) * 256)
            kc, vc = kcat.at[unit], vcat.at[unit]
            kc[0:QLEN] = rows[at, HALF + hg * 256 : HALF + (hg + 1) * 256]
            vc[0:QLEN] = rows[at, 2 * HALF + hg * 256 : 2 * HALF + (hg + 1) * 256]
            if side == 0:
                kc[QLEN : QLEN + MEM] = keys_ref[0, 0, :, lanes]
                vc[QLEN : QLEN + MEM] = values_ref[0, 0, :, lanes]
                d_out = d_ref[0, 0, :, lanes]
            else:
                kc[QLEN : QLEN + MEM] = packed_ref[0, K_AT : K_AT + MEM, lanes]
                vc[QLEN : QLEN + MEM] = packed_ref[0, V_AT : V_AT + MEM, lanes]
                d_out = packed_ref[0, 0:QLEN, lanes]
            keys, values = kc[...], vc[...]
            query = jnp.concatenate([rows[at, lanes]] * 4, axis=0) * mask_q[...]
            d_rows = jnp.concatenate([d_out] * 4, axis=0) * mask_d[...]
            scores = jnp.where(live, dot(query, keys, NT), -1e30)
            d_prob = dot(d_rows, values, NT)
            expo = jnp.exp(scores - jnp.max(scores, axis=1, keepdims=True))
            prob = expo * (1.0 / jnp.sum(expo, axis=1, keepdims=True))
            inner = jnp.sum(d_prob * prob, axis=1, keepdims=True)
            prob_b = prob.astype(BF16)
            d_scores = (prob * (d_prob - inner)).astype(BF16)
            context = diagonal(dot(prob_b, values)).astype(BF16)
            if side == 0:
                ctx_own[0, :, lanes] = context
            else:
                ctx_oth[0, :, lanes] = context
            grads = (
                diagonal(dot(d_scores, keys)) * FOLD,
                dot(d_scores[:, 0:QLEN], query, TN),
                dot(prob_b[:, 0:QLEN], d_rows, TN),
            )
            for part, grad in enumerate(grads):
                for tt in range(2):
                    cb, t = divmod(part * 8 + hg * 2 + tt, 3)
                    for r in range(2):
                        k = (2 * question + r) * COL_BLOCKS + cb
                        grad_ref[k, t * 16 : (t + 1) * 16, :] += grad[
                            r * 16 : (r + 1) * 16, tt * 128 : (tt + 1) * 128
                        ]


def split_rows(value):
    high = value.astype(BF16).astype(F32)
    low = lax.broadcasted_iota(jnp.int32, value.shape, 1) < 64
    return jnp.where(low, high, value - high).astype(BF16)


def finish_grad(recv_ref, pre_ref, rate_ref, pair_ref, out_ref, cubed_ref):
    grad = jnp.sum(recv_ref[...], axis=0)
    rate = rate_ref[...]
    product = grad * pre_ref[...]
    product = product[0:16] + product[16:32] + product[32:48]
    d_rate = jnp.sum(product, axis=1, keepdims=True)
    cubed_ref[...] = split_rows(d_rate * rate * rate * rate)
    d_pre = (grad * jnp.concatenate([rate] * 3, axis=0)).astype(BF16)
    for g in range(4):
        out_ref[g, 0:CHUNK] = d_pre
        out_ref[g, CHUNK:] = pair_ref[...]


def spread(recv_ref, cubed_ref, out_ref):
    for k in range(CHIPS):
        for g in range(4):
            out_ref[k, g * CHUNK : (g + 1) * CHUNK] = recv_ref[g, 0:CHUNK]
        out_ref[k, 4 * CHUNK :] = cubed_ref[...]


def weight_grads(
    group, recv_ref, groups_ref, gains_ref, wc_ref, own_ref, send_ref, small_ref, d_in, d_pre
):
    pairs = jnp.concatenate([groups_ref[g, CHUNK:] for g in range(4)], axis=0).astype(F32)
    scaled_t = (pairs * gains_ref[...]).T.astype(BF16)
    for cb in range(COL_BLOCKS):
        for rb in range(4):
            for g in range(4):
                for t in range(3):
                    d_pre[
                        cb, g * ROWS + rb * 16 : g * ROWS + (rb + 1) * 16, t * 128 : (t + 1) * 128
                    ] = recv_ref[
                        rb * COL_BLOCKS + cb, g * CHUNK + t * 16 : g * CHUNK + (t + 1) * 16, :
                    ]
        block = d_pre[cb]
        at = slice(cb * 384, (cb + 1) * 384)
        d_w = dot(scaled_t, block)
        own_ref[:, at] = d_w[0:FEATS]
        send_ref[:, at] = d_w[FEATS:].astype(BF16)
        term = dot(block, wc_ref[:, at], NT)
        if cb == 0:
            d_in[...] = term
        else:
            d_in[...] += term
    cubed = []
    for rb in range(4):
        total = jnp.zeros((16, 128), F32)
        for cb in range(COL_BLOCKS):
            total += recv_ref[rb * COL_BLOCKS + cb, 4 * CHUNK :].astype(F32)
        cubed.append(total[:, 0:1] + total[:, 64:65])
    cubed = jnp.broadcast_to(jnp.concatenate(cubed, axis=0), (ROWS, 128))
    mine = d_in[pl.ds(pl.multiple_of(group[0] * ROWS, ROWS), ROWS), :]
    d_gain = jnp.sum(pairs * d_in[...], axis=0, keepdims=True)
    low = lax.broadcasted_iota(jnp.int32, (ROWS, 128), 1) < 64
    small_ref[0, 0:ROWS] = mine
    small_ref[0, ROWS : ROWS + 8] = jnp.broadcast_to(d_gain, (8, 128))
    small_ref[1, 0:ROWS] = jnp.where(low, cubed, mine)
    small_ref[1, ROWS : ROWS + 8] = jnp.broadcast_to(d_gain, (8, 128))


def write_weight(core, own_ref, recv_ref, out_ref):
    half = pl.program_id(0) % 2

    @pl.when(half == core[0])
    def _():
        out_ref[...] = own_ref[...]

    @pl.when(half != core[0])
    def _():
        out_ref[...] = recv_ref[...].astype(F32)


def finish_small(small_ref, recv_ref, q_ref, gain_ref, dq_ref, dg_ref):
    d_input = small_ref[0:ROWS, 0:FEATS] + recv_ref[0:ROWS, 64:128]
    cubed = small_ref[ROWS + 8 :, 0:1] + recv_ref[0:ROWS, 0:1]
    question = q_ref[...].astype(F32)
    gain = gain_ref[...].astype(F32)
    dq_ref[...] = (gain * d_input - cubed * question / D).astype(BF16)
    dg_ref[...] = small_ref[ROWS : ROWS + 1, 0:FEATS] + recv_ref[ROWS : ROWS + 1, 64:128]


def call(body, outs, specs, scratch=()):
    return pl.pallas_call(
        body,
        out_shape=[jax.ShapeDtypeStruct(s, t) for s, t in outs],
        in_specs=specs,
        out_specs=[VMEM] * len(outs),
        scratch_shapes=list(scratch),
        compiler_params=PARAMS,
    )


def shards(question, norm_gain, w_qkv, mem_keys, mem_values, mem_length, owner, d_context):
    position = lax.axis_index("passage")
    core = jnp.reshape(position % 2, (1,)).astype(jnp.int32)
    group = jnp.reshape(lax.axis_index("dp"), (1,)).astype(jnp.int32)
    swap = [(i, i ^ 1) for i in range(2 * CHIPS)]
    same_core = [[c + 2 * i for i in range(CHIPS)] for c in range(2)]

    def exchange(x):
        return lax.all_to_all(x, "passage", 0, 0, tiled=True, axis_index_groups=same_core)

    q64 = question.reshape(ROWS, FEATS)
    gain = norm_gain.reshape(1, FEATS)

    (sent,) = call(pack_w, [((80, COLS), BF16)], [SMEM] + [VMEM] * 3)(core, w_qkv, q64, gain)
    recv = lax.ppermute(sent, "passage", swap)

    info = jnp.concatenate([mem_length.reshape(4), owner.reshape(4)])
    other_info = lax.ppermute(info, "passage", swap)
    packed = pl.pallas_call(
        pack_memory,
        out_shape=jax.ShapeDtypeStruct((4, PACKED, HALF), BF16),
        grid_spec=pltpu.PrefetchScalarGridSpec(
            num_scalar_prefetch=1,
            grid=(4,),
            in_specs=[
                pl.BlockSpec((1, 1, MEM, HALF), lambda s, c: (s // 2, s % 2, 0, 1 - c[0])),
                pl.BlockSpec((1, 1, MEM, HALF), lambda s, c: (s // 2, s % 2, 0, 1 - c[0])),
                pl.BlockSpec((1, 1, QLEN, HALF), lambda s, c: (s // 2, s % 2, 0, 1 - c[0])),
            ],
            out_specs=pl.BlockSpec((1, PACKED, HALF), lambda s, c: (s, 0, 0)),
        ),
        compiler_params=PARAMS,
    )(core, mem_keys, mem_values, d_context)
    packed = lax.ppermute(packed, "passage", swap)

    part, wc, pair, gains = call(
        project,
        [
            ((CHIPS, CHUNK + 8, 128), F32),
            ((2 * FEATS, COLS), BF16),
            ((ROWS, 2 * FEATS), BF16),
            ((1, 2 * FEATS), F32),
        ],
        [SMEM] + [VMEM] * 4,
    )(core, w_qkv, q64, gain, recv)
    part = exchange(part)
    qkv, pre, rate = call(
        normalise,
        [((CHIPS, CHUNK, 128), BF16), ((CHUNK, 128), F32), ((16, 128), F32)],
        [VMEM],
    )(part)
    qkv = exchange(qkv)

    own_info = jnp.concatenate([info, core])
    ctx_own, ctx_oth, grads = pl.pallas_call(
        attend,
        out_shape=[
            jax.ShapeDtypeStruct((4, QLEN, HALF), BF16),
            jax.ShapeDtypeStruct((4, QLEN, HALF), BF16),
            jax.ShapeDtypeStruct((CHIPS, CHUNK, 128), F32),
        ],
        grid_spec=pltpu.PrefetchScalarGridSpec(
            num_scalar_prefetch=2,
            grid=(4,),
            in_specs=[
                pl.BlockSpec((CHIPS, CHUNK, 128), lambda s, c, o: (0, 0, 0)),
                pl.BlockSpec((1, 1, MEM, HALF), lambda s, c, o: (s // 2, s % 2, 0, c[8])),
                pl.BlockSpec((1, 1, MEM, HALF), lambda s, c, o: (s // 2, s % 2, 0, c[8])),
                pl.BlockSpec((1, 1, QLEN, HALF), lambda s, c, o: (s // 2, s % 2, 0, c[8])),
                pl.BlockSpec((1, PACKED, HALF), lambda s, c, o: (s, 0, 0)),
            ],
            out_specs=[
                pl.BlockSpec((1, QLEN, HALF), lambda s, c, o: (s, 0, 0)),
                pl.BlockSpec((1, QLEN, HALF), lambda s, c, o: (s, 0, 0)),
                pl.BlockSpec((CHIPS, CHUNK, 128), lambda s, c, o: (0, 0, 0)),
            ],
            scratch_shapes=[
                pltpu.VMEM((ROWS, COLS), BF16),
                pltpu.VMEM((128, 256), BF16),
                pltpu.VMEM((128, 256), BF16),
                pltpu.VMEM((8, 256, 256), BF16),
                pltpu.VMEM((8, 256, 256), BF16),
            ],
        ),
        compiler_params=PARAMS,
    )(own_info, other_info, qkv, mem_keys, mem_values, d_context, packed)
    ctx_mine = lax.ppermute(ctx_oth, "passage", swap)
    first = core[0] == 0
    context = jnp.concatenate(
        [jnp.where(first, ctx_own, ctx_mine), jnp.where(first, ctx_mine, ctx_own)], axis=-1
    )

    grads = exchange(grads)
    chunk, cubed = call(
        finish_grad,
        [((4, CHUNK + ROWS, 128), BF16), ((16, 128), BF16)],
        [VMEM] * 4,
    )(grads, pre, rate, pair)
    groups = lax.all_to_all(chunk, "dp", 0, 0, tiled=True)
    (d_pre,) = call(spread, [((CHIPS, 4 * CHUNK + 16, 128), BF16)], [VMEM] * 2)(groups, cubed)
    d_pre = exchange(d_pre)
    own_w, send_w, small = call(
        weight_grads,
        [((FEATS, COLS), F32), ((FEATS, COLS), BF16), ((2, ROWS + 8, 128), F32)],
        [SMEM] + [VMEM] * 4,
        [pltpu.VMEM((4 * ROWS, 128), F32), pltpu.VMEM((COL_BLOCKS, 4 * ROWS, 384), BF16)],
    )(group, d_pre, groups, gains, wc)
    recv_w = lax.ppermute(send_w, "passage", swap)
    recv_small = lax.ppermute(small[1], "passage", swap)
    own_small = jnp.concatenate([small[0], small[1, 0:ROWS]], axis=0)
    d_question, d_gain = call(
        finish_small, [((ROWS, FEATS), BF16), ((1, FEATS), F32)], [VMEM] * 4
    )(own_small, recv_small, q64, gain)
    d_weight = pl.pallas_call(
        write_weight,
        out_shape=jax.ShapeDtypeStruct((FEATS, 2 * COLS), F32),
        grid_spec=pltpu.PrefetchScalarGridSpec(
            num_scalar_prefetch=1,
            grid=(6,),
            in_specs=[
                pl.BlockSpec((FEATS, HALF), lambda j, c: (0, j // 2)),
                pl.BlockSpec((FEATS, HALF), lambda j, c: (0, j // 2)),
            ],
            out_specs=pl.BlockSpec((FEATS, HALF), lambda j, c: (0, j)),
        ),
        compiler_params=PARAMS,
    )(core, own_w, recv_w)
    return (
        context.reshape(2, 2, QLEN, 2 * HALF),
        d_question.reshape(question.shape),
        d_gain.reshape(norm_gain.shape),
        d_weight,
    )


def solution(mesh):
    return jax.shard_map(
        shards,
        mesh=mesh,
        in_specs=(
            P("dp", None, "passage"),
            P("passage"),
            P("passage", None),
            P("passage", "dp", None, None),
            P("passage", "dp", None, None),
            P("passage", "dp"),
            P("passage", "dp", None),
            P("passage", "dp", None, None),
        ),
        out_specs=(
            P("passage", "dp", None, None),
            P("dp", None, "passage"),
            P("passage"),
            P("passage", None),
        ),
        check_vma=False,
    )
```

```python
import functools

import jax
import jax.numpy as jnp
from jax import lax
from jax.experimental import pallas as pl
from jax.experimental.pallas import tpu as pltpu
from jax.sharding import PartitionSpec as P

D = 4096
EPS = 1e-06
QLEN = 32
ROWS = 64
FEATS = 64
MEM = 200
HALF = 1024
COLS = 3 * HALF
CHIPS = 32
COL_BLOCKS = 8
CHUNK = 48
K_AT, V_AT, PACKED = 32, 240, 448
FOLD = 0.125

BF16 = jnp.bfloat16
F32 = jnp.float32
VMEM = pl.BlockSpec(memory_space=pltpu.VMEM)
SMEM = pl.BlockSpec(memory_space=pltpu.SMEM)
PARAMS = pltpu.CompilerParams(vmem_limit_bytes=24 * 1024 * 1024)
WIDE = pltpu.CompilerParams(vmem_limit_bytes=60 * 1024 * 1024)

NT = (((1,), (1,)), ((), ()))
TN = (((0,), (0,)), ((), ()))


def dot(a, b, dims=(((1,), (0,)), ((), ()))):
    return lax.dot_general(a, b, dims, preferred_element_type=F32)


def lanes_of(index, width):
    return pl.ds(pl.multiple_of(index * width, width), width)


def pack_w(core, length, owner, w_ref, q_ref, gain_ref, mine_ref, out_ref, info_ref):
    lane = lax.broadcasted_iota(jnp.int32, (16, 128), 1)
    values = jnp.zeros((16, 128), F32)
    for s in range(4):
        for kind, value in enumerate((length[s // 2, s % 2], owner[s // 2, 0, s % 2])):
            info_ref[4 * kind + s] = value
            values = jnp.where(lane == 4 * kind + s, value.astype(F32), values)
    info_ref[8] = core[0]
    for ref, half in ((out_ref, 1 - core[0]), (mine_ref, core[0])):
        for b in range(3):
            ref[0:FEATS, b * HALF : (b + 1) * HALF] = w_ref[:, lanes_of(2 * b + half, HALF)]
        for j in range(4):
            ref[64:80, j * 128 : j * 128 + 64] = q_ref[j * 16 : (j + 1) * 16, :]
        ref[64:80, 512:576] = jnp.broadcast_to(gain_ref[...], (16, FEATS))
        ref[64:80, 640:768] = values.astype(BF16)


def pack_memory(core, keys_ref, values_ref, d_ref, out_ref):
    out_ref[0, 0:QLEN] = d_ref[0, 0]
    out_ref[0, K_AT : K_AT + MEM] = keys_ref[0, 0]
    out_ref[0, V_AT : V_AT + MEM] = values_ref[0, 0]


def unpack(ref):
    question = [ref[64:80, j * 128 : j * 128 + 64].astype(F32) for j in range(4)]
    return jnp.concatenate(question, axis=0), ref[64:80, 512:576].astype(F32)[0:1]


def slots_of(recv_ref, info_ref):
    values = recv_ref[64:80, 640:768].astype(F32)[0:1]
    lane = lax.broadcasted_iota(jnp.int32, (1, 128), 1)
    for i in range(8):
        info_ref[i] = jnp.sum(jnp.where(lane == i, values, 0.0)).astype(jnp.int32)


def project(mine_ref, recv_ref, part_ref, wc_ref, pair_ref, gains_ref):
    question, gain = unpack(mine_ref)
    their_question, their_gain = unpack(recv_ref)
    pair = jnp.concatenate([question, their_question], axis=1)
    gains = jnp.concatenate([gain, their_gain], axis=1)
    pair_ref[...] = pair.astype(BF16)
    gains_ref[...] = gains
    scaled = (pair * gains).astype(BF16)
    wc_ref[0:FEATS, :] = mine_ref[0:FEATS, :]
    wc_ref[FEATS:, :] = recv_ref[0:FEATS, :]
    for cb in range(COL_BLOCKS):
        pre = dot(scaled, wc_ref[:, cb * 384 : (cb + 1) * 384])
        for rb in range(4):
            for t in range(3):
                part_ref[rb * COL_BLOCKS + cb, t * 16 : (t + 1) * 16, :] = pre[
                    rb * 16 : (rb + 1) * 16, t * 128 : (t + 1) * 128
                ]
    squares = jnp.sum(pair * pair, axis=1, keepdims=True)
    low = lax.broadcasted_iota(jnp.int32, (8, 128), 1) < 64
    for rb in range(4):
        tile = jnp.where(
            low, squares[rb * 16 : rb * 16 + 8], squares[rb * 16 + 8 : rb * 16 + 16]
        )
        for cb in range(COL_BLOCKS):
            part_ref[rb * COL_BLOCKS + cb, CHUNK : CHUNK + 8, :] = tile


def normalise(part_ref, qkv_ref, pre_ref, rate_ref):
    total = jnp.sum(part_ref[...], axis=0)
    rates = lax.rsqrt(total[CHUNK:] / D + EPS)
    rate = jnp.concatenate([rates[:, 0:1], rates[:, 64:65]], axis=0)
    rate = jnp.broadcast_to(rate, (16, 128))
    pre = total[:CHUNK]
    pre_ref[...] = pre
    rate_ref[...] = rate
    qkv = (pre * jnp.concatenate([rate] * 3, axis=0)).astype(BF16)
    for k in range(CHIPS):
        qkv_ref[k] = qkv


def attend(
    own, oth, qkv_ref, keys_ref, values_ref, d_ref, packed_ref, ctx_own, ctx_oth, grad_ref,
    rows, mask_q, mask_d, kcat, vcat, query, d_rows, scores, d_prob, prob_b, d_scores, total,
):
    step = pl.program_id(0)

    @pl.when(step == 0)
    def _():
        for k in range(CHIPS):
            rb, cb = divmod(k, COL_BLOCKS)
            for t in range(3):
                at = (cb * 3 + t) * 128
                rows[rb * 16 : (rb + 1) * 16, at : at + 128] = qkv_ref[k, t * 16 : (t + 1) * 16, :]
        total[...] = jnp.zeros_like(total)
        head = lax.broadcasted_iota(jnp.int32, (128, 256), 0) // QLEN
        lane = lax.broadcasted_iota(jnp.int32, (128, 256), 1) // 64
        same = jnp.where(head == lane, 1.0, 0.0)
        mask_d[...] = same.astype(BF16)
        mask_q[...] = (same * FOLD).astype(BF16)
        for unit in range(8):
            kcat[unit, 224:256] = jnp.zeros((32, 256), BF16)
            vcat[unit, 224:256] = jnp.zeros((32, 256), BF16)

    key_at = lax.broadcasted_iota(jnp.int32, (1, 256), 1)
    lane_head = lax.broadcasted_iota(jnp.int32, (QLEN, 256), 1) // 64

    def diagonal(full):
        out = full[0:QLEN]
        for h in range(1, 4):
            out = jnp.where(lane_head == h, full[h * QLEN : (h + 1) * QLEN], out)
        return out

    units = [(side, hg) for side in range(2) for hg in range(4)]
    infos = (own, oth)
    for side, hg in units:
        info = infos[side]
        at = pl.ds(pl.multiple_of(info[4 + step] * QLEN, QLEN), QLEN)
        unit = side * 4 + hg
        lanes = slice(hg * 256, (hg + 1) * 256)
        kc, vc = kcat.at[unit], vcat.at[unit]
        kc[0:QLEN] = rows[at, HALF + hg * 256 : HALF + (hg + 1) * 256]
        vc[0:QLEN] = rows[at, 2 * HALF + hg * 256 : 2 * HALF + (hg + 1) * 256]
        if side == 0:
            kc[QLEN : QLEN + MEM] = keys_ref[0, 0, :, lanes]
            vc[QLEN : QLEN + MEM] = values_ref[0, 0, :, lanes]
            d_out = d_ref[0, 0, :, lanes]
        else:
            kc[QLEN : QLEN + MEM] = packed_ref[0, K_AT : K_AT + MEM, lanes]
            vc[QLEN : QLEN + MEM] = packed_ref[0, V_AT : V_AT + MEM, lanes]
            d_out = packed_ref[0, 0:QLEN, lanes]
        query[unit] = jnp.concatenate([rows[at, lanes]] * 4, axis=0) * mask_q[...]
        d_rows[unit] = jnp.concatenate([d_out] * 4, axis=0) * mask_d[...]
    for side, hg in units:
        unit = side * 4 + hg
        scores[unit] = dot(query[unit], kcat[unit], NT)
        d_prob[unit] = dot(d_rows[unit], vcat[unit], NT)
    for side, hg in units:
        unit = side * 4 + hg
        live = key_at < infos[side][step] + QLEN
        for h in range(4):
            part = slice(h * QLEN, (h + 1) * QLEN)
            score = jnp.where(live, scores[unit, part], -1e30)
            expo = jnp.exp(score - jnp.max(score, axis=1, keepdims=True))
            prob = expo * (1.0 / jnp.sum(expo, axis=1, keepdims=True))
            d_p = d_prob[unit, part]
            inner = jnp.sum(d_p * prob, axis=1, keepdims=True)
            prob_b[unit, part] = prob.astype(BF16)
            d_scores[unit, part] = (prob * (d_p - inner)).astype(BF16)
    for side, hg in units:
        unit = side * 4 + hg
        lanes = slice(hg * 256, (hg + 1) * 256)
        question = infos[side][4 + step]
        context = diagonal(dot(prob_b[unit], vcat[unit])).astype(BF16)
        if side == 0:
            ctx_own[0, :, lanes] = context
        else:
            ctx_oth[0, :, lanes] = context
        grads = (
            diagonal(dot(d_scores[unit], kcat[unit])) * FOLD,
            dot(d_scores[unit, :, 0:QLEN], query[unit], TN),
            dot(prob_b[unit, :, 0:QLEN], d_rows[unit], TN),
        )
        for kind, grad in enumerate(grads):
            for tt in range(2):
                cb, t = divmod(kind * 8 + hg * 2 + tt, 3)
                for r in range(2):
                    k = (2 * question + r) * COL_BLOCKS + cb
                    total[k, t * 16 : (t + 1) * 16, :] += grad[
                        r * 16 : (r + 1) * 16, tt * 128 : (tt + 1) * 128
                    ]

    @pl.when(step == 3)
    def _():
        grad_ref[...] = total[...].astype(BF16)


def join_context(core, own_ref, theirs_ref, out_ref):
    out_ref[:, :, lanes_of(core[0], HALF)] = own_ref[...]
    out_ref[:, :, lanes_of(1 - core[0], HALF)] = theirs_ref[...]


def split_rows(value):
    high = value.astype(BF16).astype(F32)
    low = lax.broadcasted_iota(jnp.int32, value.shape, 1) < 64
    return jnp.where(low, high, value - high).astype(BF16)


def finish_grad(recv_ref, pre_ref, rate_ref, pair_ref, out_ref, cubed_ref):
    grad = jnp.sum(recv_ref[...].astype(F32), axis=0)
    rate = rate_ref[...]
    product = grad * pre_ref[...]
    product = product[0:16] + product[16:32] + product[32:48]
    d_rate = jnp.sum(product, axis=1, keepdims=True)
    cubed_ref[...] = split_rows(d_rate * rate * rate * rate)
    out_ref[0, 0:CHUNK] = (grad * jnp.concatenate([rate] * 3, axis=0)).astype(BF16)
    out_ref[0, CHUNK:] = pair_ref[...]


def spread(first_ref, second_ref, cubed_ref, out_ref):
    for k in range(CHIPS):
        for g in range(4):
            ref = first_ref if g < 2 else second_ref
            out_ref[k, g * CHUNK : (g + 1) * CHUNK] = ref[g % 2, 0:CHUNK]
        out_ref[k, 4 * CHUNK :] = cubed_ref[...]


def weight_grads(
    recv_ref, first_ref, second_ref, gains_ref, wc_ref, send_ref, small_ref, d_pre, scaled, d_in
):
    pairs = [ref[g, CHUNK:] for ref in (first_ref, second_ref) for g in range(2)]
    pairs = jnp.concatenate(pairs, axis=0).astype(F32)
    scaled_t = (pairs * gains_ref[...]).T.astype(BF16)
    scaled[...] = scaled_t[0:FEATS]
    for cb in range(COL_BLOCKS):
        for rb in range(4):
            for g in range(4):
                for t in range(3):
                    d_pre[
                        cb, g * ROWS + rb * 16 : g * ROWS + (rb + 1) * 16, t * 128 : (t + 1) * 128
                    ] = recv_ref[
                        rb * COL_BLOCKS + cb, g * CHUNK + t * 16 : g * CHUNK + (t + 1) * 16, :
                    ]
        block = d_pre[cb]
        at = slice(cb * 384, (cb + 1) * 384)
        send_ref[0:FEATS, at] = dot(scaled_t[FEATS:], block).astype(BF16)
        term = dot(block, wc_ref[:, at], NT)
        if cb == 0:
            d_in[...] = term
        else:
            d_in[...] += term
    cubed = []
    for rb in range(4):
        total = jnp.zeros((16, 128), F32)
        for cb in range(COL_BLOCKS):
            total += recv_ref[rb * COL_BLOCKS + cb, 4 * CHUNK :].astype(F32)
        cubed.append(total[:, 0:1] + total[:, 64:65])
    cubed = jnp.broadcast_to(jnp.concatenate(cubed, axis=0), (ROWS, 128))
    mine = d_in[0:ROWS]
    d_gain = jnp.broadcast_to(jnp.sum(pairs * d_in[...], axis=0, keepdims=True), (16, 128))
    low = lax.broadcasted_iota(jnp.int32, (ROWS, 128), 1) < 64
    small_ref[0:ROWS] = mine
    small_ref[ROWS : 2 * ROWS] = cubed
    small_ref[2 * ROWS :] = d_gain
    for value, at in ((jnp.where(low, cubed, mine), slice(0, 64)), (d_gain, slice(64, 80))):
        high = value.astype(BF16)
        send_ref[at, COLS : COLS + 128] = high
        send_ref[at, COLS + 128 : COLS + 256] = (value - high.astype(F32)).astype(BF16)


def columns_out(half, held, dw_ref, sems):
    return [
        pltpu.make_async_copy(
            held.at[:, pl.ds(b * HALF, HALF)],
            dw_ref.at[:, lanes_of(2 * b + half, HALF)],
            sems.at[b],
        )
        for b in range(3)
    ]


def own_weight(core, d_pre_ref, scaled_ref, dw_ref, held, sems):
    for cb in range(COL_BLOCKS):
        held[:, cb * 384 : (cb + 1) * 384] = dot(scaled_ref[...], d_pre_ref[cb])
    copies = columns_out(core[0], held, dw_ref, sems)
    for copy in copies:
        copy.start()
    for copy in copies:
        copy.wait()


def finish(core, recv_ref, small_ref, mine_ref, in_ref, dq_ref, dg_ref, dw_ref, held, sems):
    copies = columns_out(1 - core[0], held, dw_ref, sems)
    for b in range(3):
        at = slice(b * HALF, (b + 1) * HALF)
        held[:, at] = recv_ref[0:FEATS, at].astype(F32)
        copies[b].start()
    theirs = recv_ref[:, COLS : COLS + 128].astype(F32)
    theirs += recv_ref[:, COLS + 128 : COLS + 256].astype(F32)
    d_input = small_ref[0:ROWS, 0:FEATS] + theirs[0:ROWS, 64:128]
    cubed = small_ref[ROWS : 2 * ROWS, 0:1] + theirs[0:ROWS, 0:1]
    question, gain = unpack(mine_ref)
    dq_ref[...] = (gain * d_input - cubed * question / D).astype(BF16)
    dg_ref[...] = small_ref[2 * ROWS : 2 * ROWS + 1, 0:FEATS] + theirs[ROWS : ROWS + 1, 64:128]
    for copy in copies:
        copy.wait()


def attention(own_info, other_info, qkv, mem_keys, mem_values, d_context, packed):
    return pl.pallas_call(
        attend,
        out_shape=[
            jax.ShapeDtypeStruct((4, QLEN, HALF), BF16),
            jax.ShapeDtypeStruct((4, QLEN, HALF), BF16),
            jax.ShapeDtypeStruct((CHIPS, CHUNK, 128), BF16),
        ],
        grid_spec=pltpu.PrefetchScalarGridSpec(
            num_scalar_prefetch=2,
            grid=(4,),
            in_specs=[
                pl.BlockSpec((CHIPS, CHUNK, 128), lambda s, c, o: (0, 0, 0)),
                pl.BlockSpec((1, 1, MEM, HALF), lambda s, c, o: (s // 2, s % 2, 0, c[8])),
                pl.BlockSpec((1, 1, MEM, HALF), lambda s, c, o: (s // 2, s % 2, 0, c[8])),
                pl.BlockSpec((1, 1, QLEN, HALF), lambda s, c, o: (s // 2, s % 2, 0, c[8])),
                pl.BlockSpec((1, PACKED, HALF), lambda s, c, o: (s, 0, 0)),
            ],
            out_specs=[
                pl.BlockSpec((1, QLEN, HALF), lambda s, c, o: (s, 0, 0)),
                pl.BlockSpec((1, QLEN, HALF), lambda s, c, o: (s, 0, 0)),
                pl.BlockSpec((CHIPS, CHUNK, 128), lambda s, c, o: (0, 0, 0)),
            ],
            scratch_shapes=[
                pltpu.VMEM((ROWS, COLS), BF16),
                pltpu.VMEM((128, 256), BF16),
                pltpu.VMEM((128, 256), BF16),
                pltpu.VMEM((8, 256, 256), BF16),
                pltpu.VMEM((8, 256, 256), BF16),
                pltpu.VMEM((8, 128, 256), BF16),
                pltpu.VMEM((8, 128, 256), BF16),
                pltpu.VMEM((8, 128, 256), F32),
                pltpu.VMEM((8, 128, 256), F32),
                pltpu.VMEM((8, 128, 256), BF16),
                pltpu.VMEM((8, 128, 256), BF16),
                pltpu.VMEM((CHIPS, CHUNK, 128), F32),
            ],
        ),
        compiler_params=WIDE,
    )(own_info, other_info, qkv, mem_keys, mem_values, d_context, packed)


def call(body, outs, specs, scratch=(), scalars=0, params=PARAMS):
    return pl.pallas_call(
        body,
        out_shape=[jax.ShapeDtypeStruct(s, t) for s, t in outs],
        in_specs=specs,
        out_specs=[VMEM] * (len(outs) - scalars) + [SMEM] * scalars,
        scratch_shapes=list(scratch),
        compiler_params=params,
    )


def shards(question, norm_gain, w_qkv, mem_keys, mem_values, mem_length, owner, d_context):
    core = jnp.reshape(lax.axis_index("passage") % 2, (1,)).astype(jnp.int32)
    swap = [(i, i ^ 1) for i in range(2 * CHIPS)]
    same_core = [[c + 2 * i for i in range(CHIPS)] for c in range(2)]

    def exchange(x):
        return lax.all_to_all(x, "passage", 0, 0, tiled=True, axis_index_groups=same_core)

    q64 = question.reshape(ROWS, FEATS)
    gain = norm_gain.reshape(1, FEATS)

    mine, sent, info = call(
        pack_w,
        [((80, COLS), BF16), ((80, COLS), BF16), ((9,), jnp.int32)],
        [SMEM] * 3 + [VMEM] * 3,
        scalars=1,
        params=WIDE,
    )(core, mem_length, owner, w_qkv, q64, gain)
    recv = lax.ppermute(sent, "passage", swap)

    memory_core, _ = lax.optimization_barrier((core, sent))
    half = lambda s, c: (s // 2, s % 2, 0, 1 - c[0])
    packed = pl.pallas_call(
        pack_memory,
        out_shape=jax.ShapeDtypeStruct((4, PACKED, HALF), BF16),
        grid_spec=pltpu.PrefetchScalarGridSpec(
            num_scalar_prefetch=1,
            grid=(4,),
            in_specs=[
                pl.BlockSpec((1, 1, MEM, HALF), half),
                pl.BlockSpec((1, 1, MEM, HALF), half),
                pl.BlockSpec((1, 1, QLEN, HALF), half),
            ],
            out_specs=pl.BlockSpec((1, PACKED, HALF), lambda s, c: (s, 0, 0)),
        ),
        compiler_params=WIDE,
    )(memory_core, mem_keys, mem_values, d_context)
    packed, recv = lax.optimization_barrier((packed, recv))
    packed = lax.ppermute(packed, "passage", swap)

    part, wc, pair, gains = call(
        project,
        [
            ((CHIPS, CHUNK + 8, 128), F32),
            ((2 * FEATS, COLS), BF16),
            ((ROWS, 2 * FEATS), BF16),
            ((1, 2 * FEATS), F32),
        ],
        [VMEM] * 2,
    )(mine, recv)
    (other_info,) = call(slots_of, [((8,), jnp.int32)], [VMEM], scalars=1)(recv)
    part = exchange(part)
    qkv, pre, rate = call(
        normalise,
        [((CHIPS, CHUNK, 128), BF16), ((CHUNK, 128), F32), ((16, 128), F32)],
        [VMEM],
    )(part)
    qkv = exchange(qkv)

    ctx_own, ctx_oth, grads = attention(
        info, other_info, qkv, mem_keys, mem_values, d_context, packed
    )
    ctx_mine = lax.ppermute(ctx_oth, "passage", swap)
    context = pl.pallas_call(
        join_context,
        out_shape=jax.ShapeDtypeStruct((4, QLEN, 2 * HALF), BF16),
        grid_spec=pltpu.PrefetchScalarGridSpec(
            num_scalar_prefetch=1,
            grid=(2,),
            in_specs=[pl.BlockSpec((2, QLEN, HALF), lambda s, c: (s, 0, 0))] * 2,
            out_specs=pl.BlockSpec((2, QLEN, 2 * HALF), lambda s, c: (s, 0, 0)),
        ),
        compiler_params=PARAMS,
    )(core, ctx_own, ctx_mine)

    grads = exchange(grads)
    chunk, cubed = call(
        finish_grad,
        [((1, CHUNK + ROWS, 128), BF16), ((16, 128), BF16)],
        [VMEM] * 4,
    )(grads, pre, rate, pair)
    first = jnp.concatenate([chunk, lax.ppermute(chunk, "dp", [(g, g ^ 1) for g in range(4)])])
    second = lax.ppermute(first, "dp", [(g, g ^ 3) for g in range(4)])
    (d_pre,) = call(spread, [((CHIPS, 4 * CHUNK + 16, 128), BF16)], [VMEM] * 3)(
        first, second, cubed
    )
    d_pre, context = lax.optimization_barrier((exchange(d_pre), context))
    send, small, blocks, scaled = call(
        weight_grads,
        [
            ((80, COLS + 256), BF16),
            ((2 * ROWS + 16, 128), F32),
            ((COL_BLOCKS, 4 * ROWS, 384), BF16),
            ((FEATS, 4 * ROWS), BF16),
        ],
        [VMEM] * 5,
        [pltpu.VMEM((4 * ROWS, 128), F32)],
    )(d_pre, first, second, gains, wc)
    recv = lax.ppermute(send, "passage", swap)
    any_space = pl.BlockSpec(memory_space=pl.ANY)
    staging = [pltpu.VMEM((FEATS, COLS), F32), pltpu.SemaphoreType.DMA((3,))]
    d_weight = pl.pallas_call(
        own_weight,
        out_shape=jax.ShapeDtypeStruct((FEATS, 2 * COLS), F32),
        in_specs=[SMEM, VMEM, VMEM],
        out_specs=any_space,
        scratch_shapes=staging,
        compiler_params=PARAMS,
    )(core, blocks, scaled)
    d_question, d_gain, d_weight = pl.pallas_call(
        finish,
        out_shape=[
            jax.ShapeDtypeStruct((ROWS, FEATS), BF16),
            jax.ShapeDtypeStruct((1, FEATS), F32),
            jax.ShapeDtypeStruct((FEATS, 2 * COLS), F32),
        ],
        in_specs=[SMEM] + [VMEM] * 3 + [any_space],
        out_specs=[VMEM, VMEM, any_space],
        scratch_shapes=staging,
        input_output_aliases={4: 2},
        compiler_params=PARAMS,
    )(core, recv, small, mine, d_weight)
    return (
        context.reshape(2, 2, QLEN, 2 * HALF),
        d_question.reshape(question.shape),
        d_gain.reshape(norm_gain.shape),
        d_weight,
    )


def solution(mesh):
    return jax.shard_map(
        shards,
        mesh=mesh,
        in_specs=(
            P("dp", None, "passage"),
            P("passage"),
            P("passage", None),
            P("passage", "dp", None, None),
            P("passage", "dp", None, None),
            P("passage", "dp"),
            P("passage", "dp", None),
            P("passage", "dp", None, None),
        ),
        out_specs=(
            P("passage", "dp", None, None),
            P("dp", None, "passage"),
            P("passage"),
            P("passage", None),
        ),
        check_vma=False,
    )
```

```python
import functools

import jax
import jax.numpy as jnp
from jax import lax
from jax.experimental import pallas as pl
from jax.experimental.pallas import tpu as pltpu
from jax.sharding import PartitionSpec as P

D = 4096
EPS = 1e-06
QLEN = 32
ROWS = 64
FEATS = 64
MEM = 200
HALF = 1024
COLS = 3 * HALF
CHIPS = 32
COL_BLOCKS = 8
CHUNK = 48
K_AT, V_AT, PACKED = 32, 240, 448
FOLD = 0.125

BF16 = jnp.bfloat16
F32 = jnp.float32
VMEM = pl.BlockSpec(memory_space=pltpu.VMEM)
SMEM = pl.BlockSpec(memory_space=pltpu.SMEM)
PARAMS = pltpu.CompilerParams(vmem_limit_bytes=24 * 1024 * 1024)
WIDE = pltpu.CompilerParams(vmem_limit_bytes=60 * 1024 * 1024)

NT = (((1,), (1,)), ((), ()))
TN = (((0,), (0,)), ((), ()))


def dot(a, b, dims=(((1,), (0,)), ((), ()))):
    return lax.dot_general(a, b, dims, preferred_element_type=F32)


def lanes_of(index, width):
    return pl.ds(pl.multiple_of(index * width, width), width)


def pack_w(core, length, owner, w_ref, q_ref, gain_ref, mine_ref, out_ref, info_ref):
    for s in range(4):
        info_ref[s] = length[s // 2, s % 2]
        info_ref[4 + s] = owner[s // 2, 0, s % 2]
    info_ref[8] = core[0]
    for ref, half in ((out_ref, 1 - core[0]), (mine_ref, core[0])):
        for b in range(3):
            ref[0:FEATS, b * HALF : (b + 1) * HALF] = w_ref[:, lanes_of(2 * b + half, HALF)]
        for j in range(4):
            ref[64:80, j * 128 : j * 128 + 64] = q_ref[j * 16 : (j + 1) * 16, :]
        ref[64:80, 512:576] = jnp.broadcast_to(gain_ref[...], (16, FEATS))


def pack_memory(core, keys_ref, values_ref, d_ref, out_ref):
    out_ref[0, 0:QLEN] = d_ref[0, 0]
    out_ref[0, K_AT : K_AT + MEM] = keys_ref[0, 0]
    out_ref[0, V_AT : V_AT + MEM] = values_ref[0, 0]


def unpack(ref):
    question = [ref[64:80, j * 128 : j * 128 + 64].astype(F32) for j in range(4)]
    return jnp.concatenate(question, axis=0), ref[64:80, 512:576].astype(F32)[0:1]


def project(mine_ref, recv_ref, part_ref, wc_ref, pair_ref, gains_ref):
    question, gain = unpack(mine_ref)
    their_question, their_gain = unpack(recv_ref)
    pair = jnp.concatenate([question, their_question], axis=1)
    gains = jnp.concatenate([gain, their_gain], axis=1)
    pair_ref[...] = pair.astype(BF16)
    gains_ref[...] = gains
    scaled = (pair * gains).astype(BF16)
    wc_ref[0:FEATS, :] = mine_ref[0:FEATS, :]
    wc_ref[FEATS:, :] = recv_ref[0:FEATS, :]
    for cb in range(COL_BLOCKS):
        pre = dot(scaled, wc_ref[:, cb * 384 : (cb + 1) * 384])
        for rb in range(4):
            for t in range(3):
                part_ref[rb * COL_BLOCKS + cb, t * 16 : (t + 1) * 16, :] = pre[
                    rb * 16 : (rb + 1) * 16, t * 128 : (t + 1) * 128
                ]
    squares = jnp.sum(pair * pair, axis=1, keepdims=True)
    lane = lax.broadcasted_iota(jnp.int32, (8, 128), 1) // 16
    tile = jnp.zeros((8, 128), F32)
    for j in range(8):
        tile = jnp.where(lane == j, squares[j * 8 : (j + 1) * 8], tile)
    for k in range(CHIPS):
        part_ref[k, CHUNK : CHUNK + 8, :] = tile


def normalise(position, part_ref, qkv_ref, rate_ref, rates_ref):
    total = jnp.sum(part_ref[...], axis=0)
    tile = lax.rsqrt(total[CHUNK:] / D + EPS)
    rates = [
        jnp.broadcast_to(
            jnp.concatenate([tile[:, j * 32 : j * 32 + 1], tile[:, j * 32 + 16 : j * 32 + 17]], axis=0),
            (16, 128),
        )
        for j in range(4)
    ]
    rate = rates[0]
    for j in range(4):
        rates_ref[j * 16 : (j + 1) * 16] = rates[j]
        rate = jnp.where(position[0] // (2 * COL_BLOCKS) == j, rates[j], rate)
    rate_ref[...] = rate
    qkv = (total[:CHUNK] * jnp.concatenate([rate] * 3, axis=0)).astype(BF16)
    for k in range(CHIPS):
        qkv_ref[k] = qkv


def attend(
    own, oth, qkv_ref, keys_ref, values_ref, d_ref, packed_ref, ctx_own, ctx_oth, grad_ref,
    rows, mask_q, mask_d, kcat, vcat, query, d_rows, scores, d_prob, prob_b, d_scores, total,
):
    step = pl.program_id(0)

    @pl.when(step == 0)
    def _():
        for k in range(CHIPS):
            rb, cb = divmod(k, COL_BLOCKS)
            for t in range(3):
                at = (cb * 3 + t) * 128
                rows[rb * 16 : (rb + 1) * 16, at : at + 128] = qkv_ref[k, t * 16 : (t + 1) * 16, :]
        total[...] = jnp.zeros_like(total)
        head = lax.broadcasted_iota(jnp.int32, (128, 256), 0) // QLEN
        lane = lax.broadcasted_iota(jnp.int32, (128, 256), 1) // 64
        same = jnp.where(head == lane, 1.0, 0.0)
        mask_d[...] = same.astype(BF16)
        mask_q[...] = (same * FOLD).astype(BF16)
        for unit in range(8):
            kcat[unit, 224:256] = jnp.zeros((32, 256), BF16)
            vcat[unit, 224:256] = jnp.zeros((32, 256), BF16)

    key_at = lax.broadcasted_iota(jnp.int32, (256, 1), 0)
    lane_head = lax.broadcasted_iota(jnp.int32, (QLEN, 256), 1) // 64

    def diagonal(full):
        out = full[0:QLEN]
        for h in range(1, 4):
            out = jnp.where(lane_head == h, full[h * QLEN : (h + 1) * QLEN], out)
        return out

    units = [(side, hg) for side in range(2) for hg in range(4)]
    infos = (own, oth)
    for side, hg in units:
        info = infos[side]
        at = pl.ds(pl.multiple_of(info[4 + step] * QLEN, QLEN), QLEN)
        unit = side * 4 + hg
        lanes = slice(hg * 256, (hg + 1) * 256)
        kc, vc = kcat.at[unit], vcat.at[unit]
        kc[0:QLEN] = rows[at, HALF + hg * 256 : HALF + (hg + 1) * 256]
        vc[0:QLEN] = rows[at, 2 * HALF + hg * 256 : 2 * HALF + (hg + 1) * 256]
        if side == 0:
            kc[QLEN : QLEN + MEM] = keys_ref[0, 0, :, lanes]
            vc[QLEN : QLEN + MEM] = values_ref[0, 0, :, lanes]
            d_out = d_ref[0, 0, :, lanes]
        else:
            kc[QLEN : QLEN + MEM] = packed_ref[0, K_AT : K_AT + MEM, lanes]
            vc[QLEN : QLEN + MEM] = packed_ref[0, V_AT : V_AT + MEM, lanes]
            d_out = packed_ref[0, 0:QLEN, lanes]
        query[unit] = jnp.concatenate([rows[at, lanes]] * 4, axis=0) * mask_q[...]
        d_rows[unit] = jnp.concatenate([d_out] * 4, axis=0) * mask_d[...]
    for side, hg in units:
        unit = side * 4 + hg
        scores[unit] = dot(kcat[unit], query[unit], NT)
        d_prob[unit] = dot(vcat[unit], d_rows[unit], NT)
    for side, hg in units:
        unit = side * 4 + hg
        live = key_at < infos[side][step] + QLEN
        score = jnp.where(live, scores[unit], -1e30)
        expo = jnp.exp(score - jnp.max(score, axis=0, keepdims=True))
        prob = expo * (1.0 / jnp.sum(expo, axis=0, keepdims=True))
        d_p = d_prob[unit]
        inner = jnp.sum(d_p * prob, axis=0, keepdims=True)
        prob_b[unit] = prob.astype(BF16)
        d_scores[unit] = (prob * (d_p - inner)).astype(BF16)
    for side, hg in units:
        unit = side * 4 + hg
        lanes = slice(hg * 256, (hg + 1) * 256)
        question = infos[side][4 + step]
        context = diagonal(dot(prob_b[unit], vcat[unit], TN)).astype(BF16)
        if side == 0:
            ctx_own[0, :, lanes] = context
        else:
            ctx_oth[0, :, lanes] = context
        grads = (
            diagonal(dot(d_scores[unit], kcat[unit], TN)) * FOLD,
            dot(d_scores[unit, 0:QLEN], query[unit]),
            dot(prob_b[unit, 0:QLEN], d_rows[unit]),
        )
        for kind, grad in enumerate(grads):
            for tt in range(2):
                cb, t = divmod(kind * 8 + hg * 2 + tt, 3)
                for r in range(2):
                    k = (2 * question + r) * COL_BLOCKS + cb
                    total[k, t * 16 : (t + 1) * 16, :] += grad[
                        r * 16 : (r + 1) * 16, tt * 128 : (tt + 1) * 128
                    ]

    @pl.when(step == 3)
    def _():
        grad_ref[...] = total[...].astype(BF16)


def join_context(core, own_ref, theirs_ref, out_ref):
    out_ref[:, :, lanes_of(core[0], HALF)] = own_ref[...]
    out_ref[:, :, lanes_of(1 - core[0], HALF)] = theirs_ref[...]


def finish_grad(recv_ref, rate_ref, pair_ref, out_ref):
    grad = jnp.sum(recv_ref[...].astype(F32), axis=0)
    out_ref[0, 0:CHUNK] = (grad * jnp.concatenate([rate_ref[...]] * 3, axis=0)).astype(BF16)
    out_ref[0, CHUNK:] = pair_ref[...]


def spread(first_ref, second_ref, out_ref):
    for k in range(CHIPS):
        for g in range(4):
            ref = first_ref if g < 2 else second_ref
            out_ref[k, g * CHUNK : (g + 1) * CHUNK] = ref[g % 2, 0:CHUNK]


def weight_grads(
    recv_ref, qkv_ref, first_ref, second_ref, gains_ref, wc_ref,
    send_ref, small_ref, d_pre, scaled, d_in,
):
    pairs = [ref[g, CHUNK:] for ref in (first_ref, second_ref) for g in range(2)]
    pairs = jnp.concatenate(pairs, axis=0).astype(F32)
    scaled_t = (pairs * gains_ref[...]).T.astype(BF16)
    scaled[...] = scaled_t[0:FEATS]
    for cb in range(COL_BLOCKS):
        for rb in range(4):
            for g in range(4):
                for t in range(3):
                    d_pre[
                        cb, g * ROWS + rb * 16 : g * ROWS + (rb + 1) * 16, t * 128 : (t + 1) * 128
                    ] = recv_ref[
                        rb * COL_BLOCKS + cb, g * CHUNK + t * 16 : g * CHUNK + (t + 1) * 16, :
                    ]
        block = d_pre[cb]
        at = slice(cb * 384, (cb + 1) * 384)
        send_ref[0:FEATS, at] = dot(scaled_t[FEATS:], block).astype(BF16)
        term = dot(block, wc_ref[:, at], NT)
        if cb == 0:
            d_in[...] = term
        else:
            d_in[...] += term
    shares = []
    for rb in range(4):
        total = jnp.zeros((16, 128), F32)
        for cb in range(COL_BLOCKS):
            k = rb * COL_BLOCKS + cb
            for t in range(3):
                at = slice(t * 16, (t + 1) * 16)
                total += recv_ref[k, at].astype(F32) * qkv_ref[k, at].astype(F32)
        shares.append(jnp.sum(total, axis=1, keepdims=True))
    share = jnp.broadcast_to(jnp.concatenate(shares, axis=0), (ROWS, 128))
    mine = d_in[0:ROWS]
    d_gain = jnp.broadcast_to(jnp.sum(pairs * d_in[...], axis=0, keepdims=True), (16, 128))
    low = lax.broadcasted_iota(jnp.int32, (ROWS, 128), 1) < 64
    small_ref[0:ROWS] = mine
    small_ref[ROWS : 2 * ROWS] = share
    small_ref[2 * ROWS :] = d_gain
    for value, at in ((jnp.where(low, share, mine), slice(0, 64)), (d_gain, slice(64, 80))):
        high = value.astype(BF16)
        send_ref[at, COLS : COLS + 128] = high
        send_ref[at, COLS + 128 : COLS + 256] = (value - high.astype(F32)).astype(BF16)


def columns_out(half, held, dw_ref, sems):
    return [
        pltpu.make_async_copy(
            held.at[:, pl.ds(b * HALF, HALF)],
            dw_ref.at[:, lanes_of(2 * b + half, HALF)],
            sems.at[b],
        )
        for b in range(3)
    ]


def own_weight(core, d_pre_ref, scaled_ref, dw_ref, held, sems):
    for cb in range(COL_BLOCKS):
        held[:, cb * 384 : (cb + 1) * 384] = dot(scaled_ref[...], d_pre_ref[cb])
    copies = columns_out(core[0], held, dw_ref, sems)
    for copy in copies:
        copy.start()
    for copy in copies:
        copy.wait()


def finish(core, recv_ref, small_ref, rates_ref, mine_ref, in_ref, dq_ref, dg_ref, dw_ref, held, sems):
    copies = columns_out(1 - core[0], held, dw_ref, sems)
    for b in range(3):
        at = slice(b * HALF, (b + 1) * HALF)
        held[:, at] = recv_ref[0:FEATS, at].astype(F32)
        copies[b].start()
    theirs = recv_ref[:, COLS : COLS + 128].astype(F32)
    theirs += recv_ref[:, COLS + 128 : COLS + 256].astype(F32)
    d_input = small_ref[0:ROWS, 0:FEATS] + theirs[0:ROWS, 64:128]
    cubed = rates_ref[:, 0:1] * (small_ref[ROWS : 2 * ROWS, 0:1] + theirs[0:ROWS, 0:1])
    question, gain = unpack(mine_ref)
    dq_ref[...] = (gain * d_input - cubed * question / D).astype(BF16)
    dg_ref[...] = small_ref[2 * ROWS : 2 * ROWS + 1, 0:FEATS] + theirs[ROWS : ROWS + 1, 64:128]
    for copy in copies:
        copy.wait()


def attention(own_info, other_info, qkv, mem_keys, mem_values, d_context, packed):
    return pl.pallas_call(
        attend,
        out_shape=[
            jax.ShapeDtypeStruct((4, QLEN, HALF), BF16),
            jax.ShapeDtypeStruct((4, QLEN, HALF), BF16),
            jax.ShapeDtypeStruct((CHIPS, CHUNK, 128), BF16),
        ],
        grid_spec=pltpu.PrefetchScalarGridSpec(
            num_scalar_prefetch=2,
            grid=(4,),
            in_specs=[
                pl.BlockSpec((CHIPS, CHUNK, 128), lambda s, c, o: (0, 0, 0)),
                pl.BlockSpec((1, 1, MEM, HALF), lambda s, c, o: (s // 2, s % 2, 0, c[8])),
                pl.BlockSpec((1, 1, MEM, HALF), lambda s, c, o: (s // 2, s % 2, 0, c[8])),
                pl.BlockSpec((1, 1, QLEN, HALF), lambda s, c, o: (s // 2, s % 2, 0, c[8])),
                pl.BlockSpec((1, PACKED, HALF), lambda s, c, o: (s, 0, 0)),
            ],
            out_specs=[
                pl.BlockSpec((1, QLEN, HALF), lambda s, c, o: (s, 0, 0)),
                pl.BlockSpec((1, QLEN, HALF), lambda s, c, o: (s, 0, 0)),
                pl.BlockSpec((CHIPS, CHUNK, 128), lambda s, c, o: (0, 0, 0)),
            ],
            scratch_shapes=[
                pltpu.VMEM((ROWS, COLS), BF16),
                pltpu.VMEM((128, 256), BF16),
                pltpu.VMEM((128, 256), BF16),
                pltpu.VMEM((8, 256, 256), BF16),
                pltpu.VMEM((8, 256, 256), BF16),
                pltpu.VMEM((8, 128, 256), BF16),
                pltpu.VMEM((8, 128, 256), BF16),
                pltpu.VMEM((8, 256, 128), F32),
                pltpu.VMEM((8, 256, 128), F32),
                pltpu.VMEM((8, 256, 128), BF16),
                pltpu.VMEM((8, 256, 128), BF16),
                pltpu.VMEM((CHIPS, CHUNK, 128), F32),
            ],
        ),
        compiler_params=WIDE,
    )(own_info, other_info, qkv, mem_keys, mem_values, d_context, packed)


def call(body, outs, specs, scratch=(), scalars=0, params=PARAMS):
    return pl.pallas_call(
        body,
        out_shape=[jax.ShapeDtypeStruct(s, t) for s, t in outs],
        in_specs=specs,
        out_specs=[VMEM] * (len(outs) - scalars) + [SMEM] * scalars,
        scratch_shapes=list(scratch),
        compiler_params=params,
    )


def shards(question, norm_gain, w_qkv, mem_keys, mem_values, mem_length, owner, d_context):
    position = jnp.reshape(lax.axis_index("passage"), (1,)).astype(jnp.int32)
    core = position % 2
    swap = [(i, i ^ 1) for i in range(2 * CHIPS)]
    same_core = [[c + 2 * i for i in range(CHIPS)] for c in range(2)]

    def exchange(x):
        return lax.all_to_all(x, "passage", 0, 0, tiled=True, axis_index_groups=same_core)

    q64 = question.reshape(ROWS, FEATS)
    gain = norm_gain.reshape(1, FEATS)

    mine, sent, info = call(
        pack_w,
        [((80, COLS), BF16), ((80, COLS), BF16), ((9,), jnp.int32)],
        [SMEM] * 3 + [VMEM] * 3,
        scalars=1,
        params=WIDE,
    )(core, mem_length, owner, w_qkv, q64, gain)
    recv, other_info = lax.optimization_barrier(
        (lax.ppermute(sent, "passage", swap), lax.ppermute(info, "passage", swap))
    )

    memory_core, _ = lax.optimization_barrier((core, sent))
    half = lambda s, c: (s // 2, s % 2, 0, 1 - c[0])
    packed = pl.pallas_call(
        pack_memory,
        out_shape=jax.ShapeDtypeStruct((4, PACKED, HALF), BF16),
        grid_spec=pltpu.PrefetchScalarGridSpec(
            num_scalar_prefetch=1,
            grid=(4,),
            in_specs=[
                pl.BlockSpec((1, 1, MEM, HALF), half),
                pl.BlockSpec((1, 1, MEM, HALF), half),
                pl.BlockSpec((1, 1, QLEN, HALF), half),
            ],
            out_specs=pl.BlockSpec((1, PACKED, HALF), lambda s, c: (s, 0, 0)),
        ),
        compiler_params=WIDE,
    )(memory_core, mem_keys, mem_values, d_context)
    packed, recv = lax.optimization_barrier((packed, recv))
    packed = lax.ppermute(packed, "passage", swap)

    part, wc, pair, gains = call(
        project,
        [
            ((CHIPS, CHUNK + 8, 128), F32),
            ((2 * FEATS, COLS), BF16),
            ((ROWS, 2 * FEATS), BF16),
            ((1, 2 * FEATS), F32),
        ],
        [VMEM] * 2,
    )(mine, recv)
    part = exchange(part)
    qkv, rate, rates = call(
        normalise,
        [((CHIPS, CHUNK, 128), BF16), ((16, 128), F32), ((ROWS, 128), F32)],
        [SMEM, VMEM],
    )(position, part)
    qkv = exchange(qkv)

    ctx_own, ctx_oth, grads = attention(
        info, other_info, qkv, mem_keys, mem_values, d_context, packed
    )
    ctx_mine = lax.ppermute(ctx_oth, "passage", swap)
    context = pl.pallas_call(
        join_context,
        out_shape=jax.ShapeDtypeStruct((4, QLEN, 2 * HALF), BF16),
        grid_spec=pltpu.PrefetchScalarGridSpec(
            num_scalar_prefetch=1,
            grid=(2,),
            in_specs=[pl.BlockSpec((2, QLEN, HALF), lambda s, c: (s, 0, 0))] * 2,
            out_specs=pl.BlockSpec((2, QLEN, 2 * HALF), lambda s, c: (s, 0, 0)),
        ),
        compiler_params=PARAMS,
    )(core, ctx_own, ctx_mine)

    grads = exchange(grads)
    (chunk,) = call(finish_grad, [((1, CHUNK + ROWS, 128), BF16)], [VMEM] * 3)(grads, rate, pair)
    first = jnp.concatenate([chunk, lax.ppermute(chunk, "dp", [(g, g ^ 1) for g in range(4)])])
    second = lax.ppermute(first, "dp", [(g, g ^ 3) for g in range(4)])
    (d_pre,) = call(spread, [((CHIPS, 4 * CHUNK, 128), BF16)], [VMEM] * 2)(first, second)
    d_pre, context = lax.optimization_barrier((exchange(d_pre), context))
    send, small, blocks, scaled = call(
        weight_grads,
        [
            ((80, COLS + 256), BF16),
            ((2 * ROWS + 16, 128), F32),
            ((COL_BLOCKS, 4 * ROWS, 384), BF16),
            ((FEATS, 4 * ROWS), BF16),
        ],
        [VMEM] * 6,
        [pltpu.VMEM((4 * ROWS, 128), F32)],
    )(d_pre, qkv, first, second, gains, wc)
    recv = lax.ppermute(send, "passage", swap)
    any_space = pl.BlockSpec(memory_space=pl.ANY)
    staging = [pltpu.VMEM((FEATS, COLS), F32), pltpu.SemaphoreType.DMA((3,))]
    d_weight = pl.pallas_call(
        own_weight,
        out_shape=jax.ShapeDtypeStruct((FEATS, 2 * COLS), F32),
        in_specs=[SMEM, VMEM, VMEM],
        out_specs=any_space,
        scratch_shapes=staging,
        compiler_params=PARAMS,
    )(core, blocks, scaled)
    d_question, d_gain, d_weight = pl.pallas_call(
        finish,
        out_shape=[
            jax.ShapeDtypeStruct((ROWS, FEATS), BF16),
            jax.ShapeDtypeStruct((1, FEATS), F32),
            jax.ShapeDtypeStruct((FEATS, 2 * COLS), F32),
        ],
        in_specs=[SMEM] + [VMEM] * 4 + [any_space],
        out_specs=[VMEM, VMEM, any_space],
        scratch_shapes=staging,
        input_output_aliases={5: 2},
        compiler_params=PARAMS,
    )(core, recv, small, rates, mine, d_weight)
    return (
        context.reshape(2, 2, QLEN, 2 * HALF),
        d_question.reshape(question.shape),
        d_gain.reshape(norm_gain.shape),
        d_weight,
    )


def solution(mesh):
    return jax.shard_map(
        shards,
        mesh=mesh,
        in_specs=(
            P("dp", None, "passage"),
            P("passage"),
            P("passage", None),
            P("passage", "dp", None, None),
            P("passage", "dp", None, None),
            P("passage", "dp"),
            P("passage", "dp", None),
            P("passage", "dp", None, None),
        ),
        out_specs=(
            P("passage", "dp", None, None),
            P("dp", None, "passage"),
            P("passage"),
            P("passage", None),
        ),
        check_vma=False,
    )
```

```python
import functools

import jax
import jax.numpy as jnp
from jax import lax
from jax.experimental import pallas as pl
from jax.experimental.pallas import tpu as pltpu
from jax.sharding import PartitionSpec as P

D = 4096
EPS = 1e-06
QLEN = 32
ROWS = 64
FEATS = 64
MEM = 200
HALF = 1024
COLS = 3 * HALF
CHIPS = 32
COL_BLOCKS = 8
CHUNK = 48
FOLD = 0.125

BF16 = jnp.bfloat16
F32 = jnp.float32
VMEM = pl.BlockSpec(memory_space=pltpu.VMEM)
SMEM = pl.BlockSpec(memory_space=pltpu.SMEM)
PARAMS = pltpu.CompilerParams(vmem_limit_bytes=24 * 1024 * 1024)
WIDE = pltpu.CompilerParams(vmem_limit_bytes=60 * 1024 * 1024)

NT = (((1,), (1,)), ((), ()))
TN = (((0,), (0,)), ((), ()))


def dot(a, b, dims=(((1,), (0,)), ((), ()))):
    return lax.dot_general(a, b, dims, preferred_element_type=F32)


def lanes_of(index, width):
    return pl.ds(pl.multiple_of(index * width, width), width)


def relay(source, stage, target, sems):
    return (
        pltpu.make_async_copy(source, stage, sems.at[0]),
        pltpu.make_async_copy(stage, target, sems.at[1]),
    )


def run_relays(relays):
    for first, _ in relays:
        first.start()
    for first, second in relays:
        first.wait()
        second.start()
    for _, second in relays:
        second.wait()


def pack_w(core, length, owner, w_ref, q_ref, gain_ref, mine_ref, out_ref, info_ref):
    for s in range(4):
        info_ref[s] = length[s // 2, s % 2]
        info_ref[4 + s] = owner[s // 2, 0, s % 2]
    info_ref[8] = core[0]
    for ref, half in ((out_ref, 1 - core[0]), (mine_ref, core[0])):
        for b in range(3):
            ref[0:FEATS, b * HALF : (b + 1) * HALF] = w_ref[:, lanes_of(2 * b + half, HALF)]
        for j in range(4):
            ref[64:80, j * 128 : j * 128 + 64] = q_ref[j * 16 : (j + 1) * 16, :]
        ref[64:80, 512:576] = jnp.broadcast_to(gain_ref[...], (16, FEATS))


def pack_memory(core, keys_hbm, values_hbm, d_hbm, out_hbm, stage, d_stage, sems):
    lanes = lanes_of(1 - core[0], HALF)
    relays = []
    for s in range(4):
        slot = (s // 2, s % 2, slice(None), lanes)
        relays += [
            relay(keys_hbm.at[slot], stage.at[s, 0], out_hbm.at[s, 0], sems.at[s, 0]),
            relay(values_hbm.at[slot], stage.at[s, 1], out_hbm.at[s, 1], sems.at[s, 1]),
            relay(d_hbm.at[slot], d_stage.at[s], out_hbm.at[s, 2, 0:QLEN], sems.at[s, 2]),
        ]
    run_relays(relays)


def unpack(ref):
    question = [ref[64:80, j * 128 : j * 128 + 64].astype(F32) for j in range(4)]
    return jnp.concatenate(question, axis=0), ref[64:80, 512:576].astype(F32)[0:1]


def project(mine_ref, recv_ref, part_ref, wc_ref, pair_ref, gains_ref):
    question, gain = unpack(mine_ref)
    their_question, their_gain = unpack(recv_ref)
    pair = jnp.concatenate([question, their_question], axis=1)
    gains = jnp.concatenate([gain, their_gain], axis=1)
    pair_ref[...] = pair.astype(BF16)
    gains_ref[...] = gains
    scaled = (pair * gains).astype(BF16)
    wc_ref[0:FEATS, :] = mine_ref[0:FEATS, :]
    wc_ref[FEATS:, :] = recv_ref[0:FEATS, :]
    for cb in range(COL_BLOCKS):
        pre = dot(scaled, wc_ref[:, cb * 384 : (cb + 1) * 384])
        for rb in range(4):
            for t in range(3):
                part_ref[rb * COL_BLOCKS + cb, t * 16 : (t + 1) * 16, :] = pre[
                    rb * 16 : (rb + 1) * 16, t * 128 : (t + 1) * 128
                ]
    squares = jnp.sum(pair * pair, axis=1, keepdims=True)
    lane = lax.broadcasted_iota(jnp.int32, (8, 128), 1) // 16
    tile = jnp.zeros((8, 128), F32)
    for j in range(8):
        tile = jnp.where(lane == j, squares[j * 8 : (j + 1) * 8], tile)
    for k in range(CHIPS):
        part_ref[k, CHUNK : CHUNK + 8, :] = tile


def normalise(position, part_ref, qkv_ref, rate_ref, rates_ref):
    total = jnp.sum(part_ref[...], axis=0)
    tile = lax.rsqrt(total[CHUNK:] / D + EPS)
    rates = [
        jnp.broadcast_to(
            jnp.concatenate([tile[:, j * 32 : j * 32 + 1], tile[:, j * 32 + 16 : j * 32 + 17]], axis=0),
            (16, 128),
        )
        for j in range(4)
    ]
    rate = rates[0]
    for j in range(4):
        rates_ref[j * 16 : (j + 1) * 16] = rates[j]
        rate = jnp.where(position[0] // (2 * COL_BLOCKS) == j, rates[j], rate)
    rate_ref[...] = rate
    qkv = (total[:CHUNK] * jnp.concatenate([rate] * 3, axis=0)).astype(BF16)
    for k in range(CHIPS):
        qkv_ref[k] = qkv


def attend(
    own, oth, qkv_ref, keys_ref, values_ref, d_ref, packed_ref, packed_d_ref, ctx_own, ctx_oth, grad_ref,
    rows, mask_q, mask_d, kcat, vcat, query, d_rows, scores, d_prob, prob_b, d_scores, total,
):
    step = pl.program_id(0)

    @pl.when(step == 0)
    def _():
        for k in range(CHIPS):
            rb, cb = divmod(k, COL_BLOCKS)
            for t in range(3):
                at = (cb * 3 + t) * 128
                rows[rb * 16 : (rb + 1) * 16, at : at + 128] = qkv_ref[k, t * 16 : (t + 1) * 16, :]
        total[...] = jnp.zeros_like(total)
        head = lax.broadcasted_iota(jnp.int32, (128, 256), 0) // QLEN
        lane = lax.broadcasted_iota(jnp.int32, (128, 256), 1) // 64
        same = jnp.where(head == lane, 1.0, 0.0)
        mask_d[...] = same.astype(BF16)
        mask_q[...] = (same * FOLD).astype(BF16)
        for unit in range(8):
            kcat[unit, 224:256] = jnp.zeros((32, 256), BF16)
            vcat[unit, 224:256] = jnp.zeros((32, 256), BF16)

    key_at = lax.broadcasted_iota(jnp.int32, (256, 1), 0)
    lane_head = lax.broadcasted_iota(jnp.int32, (QLEN, 256), 1) // 64

    def diagonal(full):
        out = full[0:QLEN]
        for h in range(1, 4):
            out = jnp.where(lane_head == h, full[h * QLEN : (h + 1) * QLEN], out)
        return out

    units = [(side, hg) for side in range(2) for hg in range(4)]
    infos = (own, oth)
    for side, hg in units:
        info = infos[side]
        at = pl.ds(pl.multiple_of(info[4 + step] * QLEN, QLEN), QLEN)
        unit = side * 4 + hg
        lanes = slice(hg * 256, (hg + 1) * 256)
        kc, vc = kcat.at[unit], vcat.at[unit]
        kc[0:QLEN] = rows[at, HALF + hg * 256 : HALF + (hg + 1) * 256]
        vc[0:QLEN] = rows[at, 2 * HALF + hg * 256 : 2 * HALF + (hg + 1) * 256]
        if side == 0:
            kc[QLEN : QLEN + MEM] = keys_ref[0, 0, :, lanes]
            vc[QLEN : QLEN + MEM] = values_ref[0, 0, :, lanes]
            d_out = d_ref[0, 0, :, lanes]
        else:
            kc[QLEN : QLEN + MEM] = packed_ref[0, 0, :, lanes]
            vc[QLEN : QLEN + MEM] = packed_ref[0, 1, :, lanes]
            d_out = packed_d_ref[0, 0, :, lanes]
        query[unit] = jnp.concatenate([rows[at, lanes]] * 4, axis=0) * mask_q[...]
        d_rows[unit] = jnp.concatenate([d_out] * 4, axis=0) * mask_d[...]
    for side, hg in units:
        unit = side * 4 + hg
        scores[unit] = dot(kcat[unit], query[unit], NT)
        d_prob[unit] = dot(vcat[unit], d_rows[unit], NT)
    for side, hg in units:
        unit = side * 4 + hg
        live = key_at < infos[side][step] + QLEN
        score = jnp.where(live, scores[unit], -1e30)
        expo = jnp.exp(score - jnp.max(score, axis=0, keepdims=True))
        prob = expo * (1.0 / jnp.sum(expo, axis=0, keepdims=True))
        d_p = d_prob[unit]
        inner = jnp.sum(d_p * prob, axis=0, keepdims=True)
        prob_b[unit] = prob.astype(BF16)
        d_scores[unit] = (prob * (d_p - inner)).astype(BF16)
    for side, hg in units:
        unit = side * 4 + hg
        lanes = slice(hg * 256, (hg + 1) * 256)
        question = infos[side][4 + step]
        context = diagonal(dot(prob_b[unit], vcat[unit], TN)).astype(BF16)
        if side == 0:
            ctx_own[0, :, lanes] = context
        else:
            ctx_oth[0, :, lanes] = context
        grads = (
            diagonal(dot(d_scores[unit], kcat[unit], TN)) * FOLD,
            dot(d_scores[unit, 0:QLEN], query[unit]),
            dot(prob_b[unit, 0:QLEN], d_rows[unit]),
        )
        for kind, grad in enumerate(grads):
            for tt in range(2):
                cb, t = divmod(kind * 8 + hg * 2 + tt, 3)
                for r in range(2):
                    k = (2 * question + r) * COL_BLOCKS + cb
                    total[k, t * 16 : (t + 1) * 16, :] += grad[
                        r * 16 : (r + 1) * 16, tt * 128 : (tt + 1) * 128
                    ]

    @pl.when(step == 3)
    def _():
        grad_ref[...] = total[...].astype(BF16)


def join_context(core, own_ref, theirs_ref, out_ref):
    out_ref[:, :, lanes_of(core[0], HALF)] = own_ref[...]
    out_ref[:, :, lanes_of(1 - core[0], HALF)] = theirs_ref[...]


def finish_grad(recv_ref, rate_ref, pair_ref, out_ref):
    grad = jnp.sum(recv_ref[...].astype(F32), axis=0)
    out_ref[0, 0:CHUNK] = (grad * jnp.concatenate([rate_ref[...]] * 3, axis=0)).astype(BF16)
    out_ref[0, CHUNK:] = pair_ref[...]


def spread(first_ref, second_ref, out_ref):
    for k in range(CHIPS):
        for g in range(4):
            ref = first_ref if g < 2 else second_ref
            out_ref[k, g * CHUNK : (g + 1) * CHUNK] = ref[g % 2, 0:CHUNK]


def weight_grads(
    recv_ref, qkv_ref, first_ref, second_ref, gains_ref, wc_ref,
    send_ref, small_ref, d_pre, scaled, d_in,
):
    pairs = [ref[g, CHUNK:] for ref in (first_ref, second_ref) for g in range(2)]
    pairs = jnp.concatenate(pairs, axis=0).astype(F32)
    scaled_t = (pairs * gains_ref[...]).T.astype(BF16)
    scaled[...] = scaled_t[0:FEATS]
    for cb in range(COL_BLOCKS):
        for rb in range(4):
            for g in range(4):
                for t in range(3):
                    d_pre[
                        cb, g * ROWS + rb * 16 : g * ROWS + (rb + 1) * 16, t * 128 : (t + 1) * 128
                    ] = recv_ref[
                        rb * COL_BLOCKS + cb, g * CHUNK + t * 16 : g * CHUNK + (t + 1) * 16, :
                    ]
        block = d_pre[cb]
        at = slice(cb * 384, (cb + 1) * 384)
        send_ref[0:FEATS, at] = dot(scaled_t[FEATS:], block).astype(BF16)
        term = dot(block, wc_ref[:, at], NT)
        if cb == 0:
            d_in[...] = term
        else:
            d_in[...] += term
    shares = []
    for rb in range(4):
        total = jnp.zeros((16, 128), F32)
        for cb in range(COL_BLOCKS):
            k = rb * COL_BLOCKS + cb
            for t in range(3):
                at = slice(t * 16, (t + 1) * 16)
                total += recv_ref[k, at].astype(F32) * qkv_ref[k, at].astype(F32)
        shares.append(jnp.sum(total, axis=1, keepdims=True))
    share = jnp.broadcast_to(jnp.concatenate(shares, axis=0), (ROWS, 128))
    mine = d_in[0:ROWS]
    d_gain = jnp.broadcast_to(jnp.sum(pairs * d_in[...], axis=0, keepdims=True), (16, 128))
    low = lax.broadcasted_iota(jnp.int32, (ROWS, 128), 1) < 64
    small_ref[0:ROWS] = mine
    small_ref[ROWS : 2 * ROWS] = share
    small_ref[2 * ROWS :] = d_gain
    for value, at in ((jnp.where(low, share, mine), slice(0, 64)), (d_gain, slice(64, 80))):
        high = value.astype(BF16)
        send_ref[at, COLS : COLS + 128] = high
        send_ref[at, COLS + 128 : COLS + 256] = (value - high.astype(F32)).astype(BF16)


def columns_out(half, held, dw_ref, sems):
    return [
        pltpu.make_async_copy(
            held.at[:, pl.ds(b * HALF, HALF)],
            dw_ref.at[:, lanes_of(2 * b + half, HALF)],
            sems.at[b],
        )
        for b in range(3)
    ]


def own_weight(core, d_pre_ref, scaled_ref, dw_ref, held, sems):
    for cb in range(COL_BLOCKS):
        held[:, cb * 384 : (cb + 1) * 384] = dot(scaled_ref[...], d_pre_ref[cb])
    copies = columns_out(core[0], held, dw_ref, sems)
    for copy in copies:
        copy.start()
    for copy in copies:
        copy.wait()


def finish(core, recv_ref, small_ref, rates_ref, mine_ref, in_ref, dq_ref, dg_ref, dw_ref, held, sems):
    copies = columns_out(1 - core[0], held, dw_ref, sems)
    for b in range(3):
        at = slice(b * HALF, (b + 1) * HALF)
        held[:, at] = recv_ref[0:FEATS, at].astype(F32)
        copies[b].start()
    theirs = recv_ref[:, COLS : COLS + 128].astype(F32)
    theirs += recv_ref[:, COLS + 128 : COLS + 256].astype(F32)
    d_input = small_ref[0:ROWS, 0:FEATS] + theirs[0:ROWS, 64:128]
    cubed = rates_ref[:, 0:1] * (small_ref[ROWS : 2 * ROWS, 0:1] + theirs[0:ROWS, 0:1])
    question, gain = unpack(mine_ref)
    dq_ref[...] = (gain * d_input - cubed * question / D).astype(BF16)
    dg_ref[...] = small_ref[2 * ROWS : 2 * ROWS + 1, 0:FEATS] + theirs[ROWS : ROWS + 1, 64:128]
    for copy in copies:
        copy.wait()


def attention(own_info, other_info, qkv, mem_keys, mem_values, d_context, packed):
    return pl.pallas_call(
        attend,
        out_shape=[
            jax.ShapeDtypeStruct((4, QLEN, HALF), BF16),
            jax.ShapeDtypeStruct((4, QLEN, HALF), BF16),
            jax.ShapeDtypeStruct((CHIPS, CHUNK, 128), BF16),
        ],
        grid_spec=pltpu.PrefetchScalarGridSpec(
            num_scalar_prefetch=2,
            grid=(4,),
            in_specs=[
                pl.BlockSpec((CHIPS, CHUNK, 128), lambda s, c, o: (0, 0, 0)),
                pl.BlockSpec((1, 1, MEM, HALF), lambda s, c, o: (s // 2, s % 2, 0, c[8])),
                pl.BlockSpec((1, 1, MEM, HALF), lambda s, c, o: (s // 2, s % 2, 0, c[8])),
                pl.BlockSpec((1, 1, QLEN, HALF), lambda s, c, o: (s // 2, s % 2, 0, c[8])),
                pl.BlockSpec((1, 2, MEM, HALF), lambda s, c, o: (s, 0, 0, 0)),
                pl.BlockSpec((1, 1, QLEN, HALF), lambda s, c, o: (s, 2, 0, 0)),
            ],
            out_specs=[
                pl.BlockSpec((1, QLEN, HALF), lambda s, c, o: (s, 0, 0)),
                pl.BlockSpec((1, QLEN, HALF), lambda s, c, o: (s, 0, 0)),
                pl.BlockSpec((CHIPS, CHUNK, 128), lambda s, c, o: (0, 0, 0)),
            ],
            scratch_shapes=[
                pltpu.VMEM((ROWS, COLS), BF16),
                pltpu.VMEM((128, 256), BF16),
                pltpu.VMEM((128, 256), BF16),
                pltpu.VMEM((8, 256, 256), BF16),
                pltpu.VMEM((8, 256, 256), BF16),
                pltpu.VMEM((8, 128, 256), BF16),
                pltpu.VMEM((8, 128, 256), BF16),
                pltpu.VMEM((8, 256, 128), F32),
                pltpu.VMEM((8, 256, 128), F32),
                pltpu.VMEM((8, 256, 128), BF16),
                pltpu.VMEM((8, 256, 128), BF16),
                pltpu.VMEM((CHIPS, CHUNK, 128), F32),
            ],
        ),
        compiler_params=WIDE,
    )(own_info, other_info, qkv, mem_keys, mem_values, d_context, packed, packed)


def call(body, outs, specs, scratch=(), scalars=0, params=PARAMS):
    return pl.pallas_call(
        body,
        out_shape=[jax.ShapeDtypeStruct(s, t) for s, t in outs],
        in_specs=specs,
        out_specs=[VMEM] * (len(outs) - scalars) + [SMEM] * scalars,
        scratch_shapes=list(scratch),
        compiler_params=params,
    )


def shards(question, norm_gain, w_qkv, mem_keys, mem_values, mem_length, owner, d_context):
    position = jnp.reshape(lax.axis_index("passage"), (1,)).astype(jnp.int32)
    core = position % 2
    swap = [(i, i ^ 1) for i in range(2 * CHIPS)]
    same_core = [[c + 2 * i for i in range(CHIPS)] for c in range(2)]

    def exchange(x):
        return lax.all_to_all(x, "passage", 0, 0, tiled=True, axis_index_groups=same_core)

    q64 = question.reshape(ROWS, FEATS)
    gain = norm_gain.reshape(1, FEATS)

    any_space = pl.BlockSpec(memory_space=pl.ANY)
    mine, sent, info = call(
        pack_w,
        [((80, COLS), BF16), ((80, COLS), BF16), ((9,), jnp.int32)],
        [SMEM] * 3 + [VMEM] * 3,
        scalars=1,
        params=WIDE,
    )(core, mem_length, owner, w_qkv, q64, gain)
    recv, other_info = lax.optimization_barrier(
        (lax.ppermute(sent, "passage", swap), lax.ppermute(info, "passage", swap))
    )

    memory_core, _ = lax.optimization_barrier((core, sent))
    packed = pl.pallas_call(
        pack_memory,
        out_shape=jax.ShapeDtypeStruct((4, 3, MEM, HALF), BF16),
        in_specs=[SMEM] + [any_space] * 3,
        out_specs=any_space,
        scratch_shapes=[
            pltpu.VMEM((4, 2, MEM, HALF), BF16),
            pltpu.VMEM((4, QLEN, HALF), BF16),
            pltpu.SemaphoreType.DMA((4, 3, 2)),
        ],
        compiler_params=WIDE,
    )(memory_core, mem_keys, mem_values, d_context)
    packed, recv = lax.optimization_barrier((packed, recv))
    packed = lax.ppermute(packed, "passage", swap)

    part, wc, pair, gains = call(
        project,
        [
            ((CHIPS, CHUNK + 8, 128), F32),
            ((2 * FEATS, COLS), BF16),
            ((ROWS, 2 * FEATS), BF16),
            ((1, 2 * FEATS), F32),
        ],
        [VMEM] * 2,
    )(mine, recv)
    part = exchange(part)
    qkv, rate, rates = call(
        normalise,
        [((CHIPS, CHUNK, 128), BF16), ((16, 128), F32), ((ROWS, 128), F32)],
        [SMEM, VMEM],
    )(position, part)
    qkv = exchange(qkv)

    ctx_own, ctx_oth, grads = attention(
        info, other_info, qkv, mem_keys, mem_values, d_context, packed
    )
    ctx_mine = lax.ppermute(ctx_oth, "passage", swap)
    context = pl.pallas_call(
        join_context,
        out_shape=jax.ShapeDtypeStruct((4, QLEN, 2 * HALF), BF16),
        grid_spec=pltpu.PrefetchScalarGridSpec(
            num_scalar_prefetch=1,
            grid=(2,),
            in_specs=[pl.BlockSpec((2, QLEN, HALF), lambda s, c: (s, 0, 0))] * 2,
            out_specs=pl.BlockSpec((2, QLEN, 2 * HALF), lambda s, c: (s, 0, 0)),
        ),
        compiler_params=PARAMS,
    )(core, ctx_own, ctx_mine)

    grads = exchange(grads)
    (chunk,) = call(finish_grad, [((1, CHUNK + ROWS, 128), BF16)], [VMEM] * 3)(grads, rate, pair)
    first = jnp.concatenate([chunk, lax.ppermute(chunk, "dp", [(g, g ^ 1) for g in range(4)])])
    second = lax.ppermute(first, "dp", [(g, g ^ 3) for g in range(4)])
    (d_pre,) = call(spread, [((CHIPS, 4 * CHUNK, 128), BF16)], [VMEM] * 2)(first, second)
    d_pre, context = lax.optimization_barrier((exchange(d_pre), context))
    send, small, blocks, scaled = call(
        weight_grads,
        [
            ((80, COLS + 256), BF16),
            ((2 * ROWS + 16, 128), F32),
            ((COL_BLOCKS, 4 * ROWS, 384), BF16),
            ((FEATS, 4 * ROWS), BF16),
        ],
        [VMEM] * 6,
        [pltpu.VMEM((4 * ROWS, 128), F32)],
    )(d_pre, qkv, first, second, gains, wc)
    recv = lax.ppermute(send, "passage", swap)
    staging = [pltpu.VMEM((FEATS, COLS), F32), pltpu.SemaphoreType.DMA((3,))]
    d_weight = pl.pallas_call(
        own_weight,
        out_shape=jax.ShapeDtypeStruct((FEATS, 2 * COLS), F32),
        in_specs=[SMEM, VMEM, VMEM],
        out_specs=any_space,
        scratch_shapes=staging,
        compiler_params=PARAMS,
    )(core, blocks, scaled)
    d_question, d_gain, d_weight = pl.pallas_call(
        finish,
        out_shape=[
            jax.ShapeDtypeStruct((ROWS, FEATS), BF16),
            jax.ShapeDtypeStruct((1, FEATS), F32),
            jax.ShapeDtypeStruct((FEATS, 2 * COLS), F32),
        ],
        in_specs=[SMEM] + [VMEM] * 4 + [any_space],
        out_specs=[VMEM, VMEM, any_space],
        scratch_shapes=staging,
        input_output_aliases={5: 2},
        compiler_params=PARAMS,
    )(core, recv, small, rates, mine, d_weight)
    return (
        context.reshape(2, 2, QLEN, 2 * HALF),
        d_question.reshape(question.shape),
        d_gain.reshape(norm_gain.shape),
        d_weight,
    )


def solution(mesh):
    return jax.shard_map(
        shards,
        mesh=mesh,
        in_specs=(
            P("dp", None, "passage"),
            P("passage"),
            P("passage", None),
            P("passage", "dp", None, None),
            P("passage", "dp", None, None),
            P("passage", "dp"),
            P("passage", "dp", None),
            P("passage", "dp", None, None),
        ),
        out_specs=(
            P("passage", "dp", None, None),
            P("dp", None, "passage"),
            P("passage"),
            P("passage", None),
        ),
        check_vma=False,
    )
```

```python
import functools

import jax
import jax.numpy as jnp
from jax import lax
from jax.experimental import pallas as pl
from jax.experimental.pallas import tpu as pltpu
from jax.sharding import PartitionSpec as P

D = 4096
EPS = 1e-06
QLEN = 32
ROWS = 64
FEATS = 64
MEM = 200
HALF = 1024
COLS = 3 * HALF
CHIPS = 32
COL_BLOCKS = 8
CHUNK = 48
FOLD = 0.125

BF16 = jnp.bfloat16
F32 = jnp.float32
VMEM = pl.BlockSpec(memory_space=pltpu.VMEM)
SMEM = pl.BlockSpec(memory_space=pltpu.SMEM)
PARAMS = pltpu.CompilerParams(vmem_limit_bytes=24 * 1024 * 1024)
WIDE = pltpu.CompilerParams(vmem_limit_bytes=60 * 1024 * 1024)

NT = (((1,), (1,)), ((), ()))
TN = (((0,), (0,)), ((), ()))


def dot(a, b, dims=(((1,), (0,)), ((), ()))):
    return lax.dot_general(a, b, dims, preferred_element_type=F32)


def lanes_of(index, width):
    return pl.ds(pl.multiple_of(index * width, width), width)


def relay(source, stage, target, sems):
    return (
        pltpu.make_async_copy(source, stage, sems.at[0]),
        pltpu.make_async_copy(stage, target, sems.at[1]),
    )


def run_relays(relays):
    for first, _ in relays:
        first.start()
    for first, second in relays:
        first.wait()
        second.start()
    for _, second in relays:
        second.wait()


def pack_w(core, length, owner, w_ref, q_ref, gain_ref, mine_ref, out_ref, info_ref):
    for s in range(4):
        info_ref[s] = length[s // 2, s % 2]
        info_ref[4 + s] = owner[s // 2, 0, s % 2]
    info_ref[8] = core[0]
    for ref, half in ((out_ref, 1 - core[0]), (mine_ref, core[0])):
        for b in range(3):
            ref[0:FEATS, b * HALF : (b + 1) * HALF] = w_ref[:, lanes_of(2 * b + half, HALF)]
        for j in range(4):
            ref[64:80, j * 128 : j * 128 + 64] = q_ref[j * 16 : (j + 1) * 16, :]
        ref[64:80, 512:576] = jnp.broadcast_to(gain_ref[...], (16, FEATS))


def pack_memory(core, keys_hbm, values_hbm, d_hbm, out_hbm, stage, d_stage, sems):
    lanes = lanes_of(1 - core[0], HALF)
    relays = []
    for s in range(4):
        slot = (s // 2, s % 2, slice(None), lanes)
        relays += [
            relay(keys_hbm.at[slot], stage.at[s, 0], out_hbm.at[s, 0], sems.at[s, 0]),
            relay(values_hbm.at[slot], stage.at[s, 1], out_hbm.at[s, 1], sems.at[s, 1]),
            relay(d_hbm.at[slot], d_stage.at[s], out_hbm.at[s, 2, 0:QLEN], sems.at[s, 2]),
        ]
    run_relays(relays)


def unpack(ref):
    question = [ref[64:80, j * 128 : j * 128 + 64].astype(F32) for j in range(4)]
    return jnp.concatenate(question, axis=0), ref[64:80, 512:576].astype(F32)[0:1]


def project(mine_ref, recv_ref, part_ref, wc_ref, pair_ref, gains_ref):
    question, gain = unpack(mine_ref)
    their_question, their_gain = unpack(recv_ref)
    pair = jnp.concatenate([question, their_question], axis=1)
    gains = jnp.concatenate([gain, their_gain], axis=1)
    pair_ref[...] = pair.astype(BF16)
    gains_ref[...] = gains
    scaled = (pair * gains).astype(BF16)
    wc_ref[0:FEATS, :] = mine_ref[0:FEATS, :]
    wc_ref[FEATS:, :] = recv_ref[0:FEATS, :]
    for cb in range(COL_BLOCKS):
        pre = dot(scaled, wc_ref[:, cb * 384 : (cb + 1) * 384])
        for rb in range(4):
            for t in range(3):
                part_ref[rb * COL_BLOCKS + cb, t * 16 : (t + 1) * 16, :] = pre[
                    rb * 16 : (rb + 1) * 16, t * 128 : (t + 1) * 128
                ]
    squares = jnp.sum(pair * pair, axis=1, keepdims=True)
    lane = lax.broadcasted_iota(jnp.int32, (8, 128), 1) // 16
    tile = jnp.zeros((8, 128), F32)
    for j in range(8):
        tile = jnp.where(lane == j, squares[j * 8 : (j + 1) * 8], tile)
    for k in range(CHIPS):
        part_ref[k, CHUNK : CHUNK + 8, :] = tile


def normalise(position, part_ref, qkv_ref, rate_ref, rates_ref):
    total = jnp.sum(part_ref[...], axis=0)
    tile = lax.rsqrt(total[CHUNK:] / D + EPS)
    rates = [
        jnp.broadcast_to(
            jnp.concatenate([tile[:, j * 32 : j * 32 + 1], tile[:, j * 32 + 16 : j * 32 + 17]], axis=0),
            (16, 128),
        )
        for j in range(4)
    ]
    rate = rates[0]
    for j in range(4):
        rates_ref[j * 16 : (j + 1) * 16] = rates[j]
        rate = jnp.where(position[0] // (2 * COL_BLOCKS) == j, rates[j], rate)
    rate_ref[...] = rate
    qkv = (total[:CHUNK] * jnp.concatenate([rate] * 3, axis=0)).astype(BF16)
    for k in range(CHIPS):
        qkv_ref[k] = qkv


def attend(
    own, oth, qkv_ref, keys_ref, values_ref, d_ref, packed_ref, packed_d_ref, ctx_own, ctx_oth, grad_ref,
    rows, mask_q, mask_d, kcat, vcat, query, d_rows, scores, d_prob, prob_b, d_scores, total,
):
    step = pl.program_id(0)

    @pl.when(step == 0)
    def _():
        for k in range(CHIPS):
            rb, cb = divmod(k, COL_BLOCKS)
            for t in range(3):
                at = (cb * 3 + t) * 128
                rows[rb * 16 : (rb + 1) * 16, at : at + 128] = qkv_ref[k, t * 16 : (t + 1) * 16, :]
        total[...] = jnp.zeros_like(total)
        head = lax.broadcasted_iota(jnp.int32, (128, 256), 0) // QLEN
        lane = lax.broadcasted_iota(jnp.int32, (128, 256), 1) // 64
        same = jnp.where(head == lane, 1.0, 0.0)
        mask_d[...] = same.astype(BF16)
        mask_q[...] = (same * FOLD).astype(BF16)
        for unit in range(8):
            kcat[unit, 224:256] = jnp.zeros((32, 256), BF16)
            vcat[unit, 224:256] = jnp.zeros((32, 256), BF16)

    key_at = lax.broadcasted_iota(jnp.int32, (256, 1), 0)
    lane_head = lax.broadcasted_iota(jnp.int32, (QLEN, 256), 1) // 64

    def diagonal(full):
        out = full[0:QLEN]
        for h in range(1, 4):
            out = jnp.where(lane_head == h, full[h * QLEN : (h + 1) * QLEN], out)
        return out

    units = [(side, hg) for side in range(2) for hg in range(4)]
    infos = (own, oth)
    for side, hg in units:
        info = infos[side]
        at = pl.ds(pl.multiple_of(info[4 + step] * QLEN, QLEN), QLEN)
        unit = side * 4 + hg
        lanes = slice(hg * 256, (hg + 1) * 256)
        kc, vc = kcat.at[unit], vcat.at[unit]
        kc[0:QLEN] = rows[at, HALF + hg * 256 : HALF + (hg + 1) * 256]
        vc[0:QLEN] = rows[at, 2 * HALF + hg * 256 : 2 * HALF + (hg + 1) * 256]
        if side == 0:
            kc[QLEN : QLEN + MEM] = keys_ref[0, 0, :, lanes]
            vc[QLEN : QLEN + MEM] = values_ref[0, 0, :, lanes]
            d_out = d_ref[0, 0, :, lanes]
        else:
            kc[QLEN : QLEN + MEM] = packed_ref[0, 0, :, lanes]
            vc[QLEN : QLEN + MEM] = packed_ref[0, 1, :, lanes]
            d_out = packed_d_ref[0, 0, :, lanes]
        query[unit] = jnp.concatenate([rows[at, lanes]] * 4, axis=0) * mask_q[...]
        d_rows[unit] = jnp.concatenate([d_out] * 4, axis=0) * mask_d[...]
    for side, hg in units:
        unit = side * 4 + hg
        scores[unit] = dot(kcat[unit], query[unit], NT)
        d_prob[unit] = dot(vcat[unit], d_rows[unit], NT)
    for side, hg in units:
        unit = side * 4 + hg
        live = key_at < infos[side][step] + QLEN
        score = jnp.where(live, scores[unit], -1e30)
        expo = jnp.exp(score - jnp.max(score, axis=0, keepdims=True))
        prob = expo * (1.0 / jnp.sum(expo, axis=0, keepdims=True))
        d_p = d_prob[unit]
        inner = jnp.sum(d_p * prob, axis=0, keepdims=True)
        prob_b[unit] = prob.astype(BF16)
        d_scores[unit] = (prob * (d_p - inner)).astype(BF16)
    for side, hg in units:
        unit = side * 4 + hg
        lanes = slice(hg * 256, (hg + 1) * 256)
        question = infos[side][4 + step]
        context = diagonal(dot(prob_b[unit], vcat[unit], TN)).astype(BF16)
        if side == 0:
            ctx_own[0, :, lanes] = context
        else:
            ctx_oth[0, :, lanes] = context
        grads = (
            diagonal(dot(d_scores[unit], kcat[unit], TN)) * FOLD,
            dot(d_scores[unit, 0:QLEN], query[unit]),
            dot(prob_b[unit, 0:QLEN], d_rows[unit]),
        )
        for kind, grad in enumerate(grads):
            for tt in range(2):
                cb, t = divmod(kind * 8 + hg * 2 + tt, 3)
                for r in range(2):
                    k = (2 * question + r) * COL_BLOCKS + cb
                    total[k, t * 16 : (t + 1) * 16, :] += grad[
                        r * 16 : (r + 1) * 16, tt * 128 : (tt + 1) * 128
                    ]

    @pl.when(step == 3)
    def _():
        grad_ref[...] = total[...].astype(BF16)


def join_context(core, own_ref, theirs_ref, out_ref):
    out_ref[:, :, lanes_of(core[0], HALF)] = own_ref[...]
    out_ref[:, :, lanes_of(1 - core[0], HALF)] = theirs_ref[...]


def finish_grad(recv_ref, rate_ref, pair_ref, out_ref):
    grad = jnp.sum(recv_ref[...].astype(F32), axis=0)
    out_ref[0, 0:CHUNK] = (grad * jnp.concatenate([rate_ref[...]] * 3, axis=0)).astype(BF16)
    out_ref[0, CHUNK:] = pair_ref[...]


def spread(at, chunks_ref, out_hbm, stage, sems):
    for g in range(2):
        stage[g * CHUNK : (g + 1) * CHUNK] = chunks_ref[g, 0:CHUNK]
    copies = [
        pltpu.make_async_copy(stage, out_hbm.at[k, at : at + 2 * CHUNK], sems.at[k])
        for k in range(CHIPS)
    ]
    for copy in copies:
        copy.start()
    for copy in copies:
        copy.wait()


def spread_first(chunks_ref, out_hbm, stage, sems):
    spread(0, chunks_ref, out_hbm, stage, sems)


def spread_second(chunks_ref, in_hbm, out_hbm, stage, sems):
    spread(2 * CHUNK, chunks_ref, out_hbm, stage, sems)


def weight_grads(
    recv_ref, qkv_ref, first_ref, second_ref, gains_ref, wc_ref,
    send_ref, small_ref, d_pre, scaled, d_in,
):
    pairs = [ref[g, CHUNK:] for ref in (first_ref, second_ref) for g in range(2)]
    pairs = jnp.concatenate(pairs, axis=0).astype(F32)
    scaled_t = (pairs * gains_ref[...]).T.astype(BF16)
    scaled[...] = scaled_t[0:FEATS]
    for cb in range(COL_BLOCKS):
        for rb in range(4):
            for g in range(4):
                for t in range(3):
                    d_pre[
                        cb, g * ROWS + rb * 16 : g * ROWS + (rb + 1) * 16, t * 128 : (t + 1) * 128
                    ] = recv_ref[
                        rb * COL_BLOCKS + cb, g * CHUNK + t * 16 : g * CHUNK + (t + 1) * 16, :
                    ]
        block = d_pre[cb]
        at = slice(cb * 384, (cb + 1) * 384)
        send_ref[0:FEATS, at] = dot(scaled_t[FEATS:], block).astype(BF16)
        term = dot(block, wc_ref[:, at], NT)
        if cb == 0:
            d_in[...] = term
        else:
            d_in[...] += term
    shares = []
    for rb in range(4):
        total = jnp.zeros((16, 128), F32)
        for cb in range(COL_BLOCKS):
            k = rb * COL_BLOCKS + cb
            for t in range(3):
                at = slice(t * 16, (t + 1) * 16)
                total += recv_ref[k, at].astype(F32) * qkv_ref[k, at].astype(F32)
        shares.append(jnp.sum(total, axis=1, keepdims=True))
    share = jnp.broadcast_to(jnp.concatenate(shares, axis=0), (ROWS, 128))
    mine = d_in[0:ROWS]
    d_gain = jnp.broadcast_to(jnp.sum(pairs * d_in[...], axis=0, keepdims=True), (16, 128))
    low = lax.broadcasted_iota(jnp.int32, (ROWS, 128), 1) < 64
    small_ref[0:ROWS] = mine
    small_ref[ROWS : 2 * ROWS] = share
    small_ref[2 * ROWS :] = d_gain
    for value, at in ((jnp.where(low, share, mine), slice(0, 64)), (d_gain, slice(64, 80))):
        high = value.astype(BF16)
        send_ref[at, COLS : COLS + 128] = high
        send_ref[at, COLS + 128 : COLS + 256] = (value - high.astype(F32)).astype(BF16)


def columns_out(half, held, dw_ref, sems):
    return [
        pltpu.make_async_copy(
            held.at[:, pl.ds(b * HALF, HALF)],
            dw_ref.at[:, lanes_of(2 * b + half, HALF)],
            sems.at[b],
        )
        for b in range(3)
    ]


def own_weight(core, d_pre_ref, scaled_ref, dw_ref, held, sems):
    for cb in range(COL_BLOCKS):
        held[:, cb * 384 : (cb + 1) * 384] = dot(scaled_ref[...], d_pre_ref[cb])
    copies = columns_out(core[0], held, dw_ref, sems)
    for copy in copies:
        copy.start()
    for copy in copies:
        copy.wait()


def finish(core, recv_ref, small_ref, rates_ref, mine_ref, in_ref, dq_ref, dg_ref, dw_ref, held, sems):
    copies = columns_out(1 - core[0], held, dw_ref, sems)
    for b in range(3):
        at = slice(b * HALF, (b + 1) * HALF)
        held[:, at] = recv_ref[0:FEATS, at].astype(F32)
        copies[b].start()
    theirs = recv_ref[:, COLS : COLS + 128].astype(F32)
    theirs += recv_ref[:, COLS + 128 : COLS + 256].astype(F32)
    d_input = small_ref[0:ROWS, 0:FEATS] + theirs[0:ROWS, 64:128]
    cubed = rates_ref[:, 0:1] * (small_ref[ROWS : 2 * ROWS, 0:1] + theirs[0:ROWS, 0:1])
    question, gain = unpack(mine_ref)
    dq_ref[...] = (gain * d_input - cubed * question / D).astype(BF16)
    dg_ref[...] = small_ref[2 * ROWS : 2 * ROWS + 1, 0:FEATS] + theirs[ROWS : ROWS + 1, 64:128]
    for copy in copies:
        copy.wait()


def attention(own_info, other_info, qkv, mem_keys, mem_values, d_context, packed):
    return pl.pallas_call(
        attend,
        out_shape=[
            jax.ShapeDtypeStruct((4, QLEN, HALF), BF16),
            jax.ShapeDtypeStruct((4, QLEN, HALF), BF16),
            jax.ShapeDtypeStruct((CHIPS, CHUNK, 128), BF16),
        ],
        grid_spec=pltpu.PrefetchScalarGridSpec(
            num_scalar_prefetch=2,
            grid=(4,),
            in_specs=[
                pl.BlockSpec((CHIPS, CHUNK, 128), lambda s, c, o: (0, 0, 0)),
                pl.BlockSpec((1, 1, MEM, HALF), lambda s, c, o: (s // 2, s % 2, 0, c[8])),
                pl.BlockSpec((1, 1, MEM, HALF), lambda s, c, o: (s // 2, s % 2, 0, c[8])),
                pl.BlockSpec((1, 1, QLEN, HALF), lambda s, c, o: (s // 2, s % 2, 0, c[8])),
                pl.BlockSpec((1, 2, MEM, HALF), lambda s, c, o: (s, 0, 0, 0)),
                pl.BlockSpec((1, 1, QLEN, HALF), lambda s, c, o: (s, 2, 0, 0)),
            ],
            out_specs=[
                pl.BlockSpec((1, QLEN, HALF), lambda s, c, o: (s, 0, 0)),
                pl.BlockSpec((1, QLEN, HALF), lambda s, c, o: (s, 0, 0)),
                pl.BlockSpec((CHIPS, CHUNK, 128), lambda s, c, o: (0, 0, 0)),
            ],
            scratch_shapes=[
                pltpu.VMEM((ROWS, COLS), BF16),
                pltpu.VMEM((128, 256), BF16),
                pltpu.VMEM((128, 256), BF16),
                pltpu.VMEM((8, 256, 256), BF16),
                pltpu.VMEM((8, 256, 256), BF16),
                pltpu.VMEM((8, 128, 256), BF16),
                pltpu.VMEM((8, 128, 256), BF16),
                pltpu.VMEM((8, 256, 128), F32),
                pltpu.VMEM((8, 256, 128), F32),
                pltpu.VMEM((8, 256, 128), BF16),
                pltpu.VMEM((8, 256, 128), BF16),
                pltpu.VMEM((CHIPS, CHUNK, 128), F32),
            ],
        ),
        compiler_params=WIDE,
    )(own_info, other_info, qkv, mem_keys, mem_values, d_context, packed, packed)


def call(body, outs, specs, scratch=(), scalars=0, params=PARAMS):
    return pl.pallas_call(
        body,
        out_shape=[jax.ShapeDtypeStruct(s, t) for s, t in outs],
        in_specs=specs,
        out_specs=[VMEM] * (len(outs) - scalars) + [SMEM] * scalars,
        scratch_shapes=list(scratch),
        compiler_params=params,
    )


def shards(question, norm_gain, w_qkv, mem_keys, mem_values, mem_length, owner, d_context):
    position = jnp.reshape(lax.axis_index("passage"), (1,)).astype(jnp.int32)
    core = position % 2
    swap = [(i, i ^ 1) for i in range(2 * CHIPS)]
    same_core = [[c + 2 * i for i in range(CHIPS)] for c in range(2)]

    def exchange(x):
        return lax.all_to_all(x, "passage", 0, 0, tiled=True, axis_index_groups=same_core)

    q64 = question.reshape(ROWS, FEATS)
    gain = norm_gain.reshape(1, FEATS)

    any_space = pl.BlockSpec(memory_space=pl.ANY)
    mine, sent, info = call(
        pack_w,
        [((80, COLS), BF16), ((80, COLS), BF16), ((9,), jnp.int32)],
        [SMEM] * 3 + [VMEM] * 3,
        scalars=1,
        params=WIDE,
    )(core, mem_length, owner, w_qkv, q64, gain)
    recv, other_info = lax.optimization_barrier(
        (lax.ppermute(sent, "passage", swap), lax.ppermute(info, "passage", swap))
    )

    memory_core, _ = lax.optimization_barrier((core, sent))
    packed = pl.pallas_call(
        pack_memory,
        out_shape=jax.ShapeDtypeStruct((4, 3, MEM, HALF), BF16),
        in_specs=[SMEM] + [any_space] * 3,
        out_specs=any_space,
        scratch_shapes=[
            pltpu.VMEM((4, 2, MEM, HALF), BF16),
            pltpu.VMEM((4, QLEN, HALF), BF16),
            pltpu.SemaphoreType.DMA((4, 3, 2)),
        ],
        compiler_params=WIDE,
    )(memory_core, mem_keys, mem_values, d_context)
    packed, recv = lax.optimization_barrier((packed, recv))
    packed = lax.ppermute(packed, "passage", swap)

    part, wc, pair, gains = call(
        project,
        [
            ((CHIPS, CHUNK + 8, 128), F32),
            ((2 * FEATS, COLS), BF16),
            ((ROWS, 2 * FEATS), BF16),
            ((1, 2 * FEATS), F32),
        ],
        [VMEM] * 2,
    )(mine, recv)
    part = exchange(part)
    qkv, rate, rates = call(
        normalise,
        [((CHIPS, CHUNK, 128), BF16), ((16, 128), F32), ((ROWS, 128), F32)],
        [SMEM, VMEM],
    )(position, part)
    qkv = exchange(qkv)

    ctx_own, ctx_oth, grads = attention(
        info, other_info, qkv, mem_keys, mem_values, d_context, packed
    )
    ctx_mine = lax.ppermute(ctx_oth, "passage", swap)
    context = pl.pallas_call(
        join_context,
        out_shape=jax.ShapeDtypeStruct((4, QLEN, 2 * HALF), BF16),
        grid_spec=pltpu.PrefetchScalarGridSpec(
            num_scalar_prefetch=1,
            grid=(2,),
            in_specs=[pl.BlockSpec((2, QLEN, HALF), lambda s, c: (s, 0, 0))] * 2,
            out_specs=pl.BlockSpec((2, QLEN, 2 * HALF), lambda s, c: (s, 0, 0)),
        ),
        compiler_params=PARAMS,
    )(core, ctx_own, ctx_mine)

    grads = exchange(grads)
    (chunk,) = call(finish_grad, [((1, CHUNK + ROWS, 128), BF16)], [VMEM] * 3)(grads, rate, pair)
    first = jnp.concatenate([chunk, lax.ppermute(chunk, "dp", [(g, g ^ 1) for g in range(4)])])
    second = lax.ppermute(first, "dp", [(g, g ^ 3) for g in range(4)])
    spaces = dict(
        out_shape=jax.ShapeDtypeStruct((CHIPS, 4 * CHUNK, 128), BF16),
        out_specs=any_space,
        scratch_shapes=[
            pltpu.VMEM((2 * CHUNK, 128), BF16),
            pltpu.SemaphoreType.DMA((CHIPS,)),
        ],
        compiler_params=PARAMS,
    )
    d_pre = pl.pallas_call(spread_first, in_specs=[VMEM], **spaces)(first)
    d_pre = pl.pallas_call(
        spread_second, in_specs=[VMEM, any_space], input_output_aliases={1: 0}, **spaces
    )(second, d_pre)
    d_pre, context = lax.optimization_barrier((exchange(d_pre), context))
    send, small, blocks, scaled = call(
        weight_grads,
        [
            ((80, COLS + 256), BF16),
            ((2 * ROWS + 16, 128), F32),
            ((COL_BLOCKS, 4 * ROWS, 384), BF16),
            ((FEATS, 4 * ROWS), BF16),
        ],
        [VMEM] * 6,
        [pltpu.VMEM((4 * ROWS, 128), F32)],
    )(d_pre, qkv, first, second, gains, wc)
    recv = lax.ppermute(send, "passage", swap)
    staging = [pltpu.VMEM((FEATS, COLS), F32), pltpu.SemaphoreType.DMA((3,))]
    d_weight = pl.pallas_call(
        own_weight,
        out_shape=jax.ShapeDtypeStruct((FEATS, 2 * COLS), F32),
        in_specs=[SMEM, VMEM, VMEM],
        out_specs=any_space,
        scratch_shapes=staging,
        compiler_params=PARAMS,
    )(core, blocks, scaled)
    d_question, d_gain, d_weight = pl.pallas_call(
        finish,
        out_shape=[
            jax.ShapeDtypeStruct((ROWS, FEATS), BF16),
            jax.ShapeDtypeStruct((1, FEATS), F32),
            jax.ShapeDtypeStruct((FEATS, 2 * COLS), F32),
        ],
        in_specs=[SMEM] + [VMEM] * 4 + [any_space],
        out_specs=[VMEM, VMEM, any_space],
        scratch_shapes=staging,
        input_output_aliases={5: 2},
        compiler_params=PARAMS,
    )(core, recv, small, rates, mine, d_weight)
    return (
        context.reshape(2, 2, QLEN, 2 * HALF),
        d_question.reshape(question.shape),
        d_gain.reshape(norm_gain.shape),
        d_weight,
    )


def solution(mesh):
    return jax.shard_map(
        shards,
        mesh=mesh,
        in_specs=(
            P("dp", None, "passage"),
            P("passage"),
            P("passage", None),
            P("passage", "dp", None, None),
            P("passage", "dp", None, None),
            P("passage", "dp"),
            P("passage", "dp", None),
            P("passage", "dp", None, None),
        ),
        out_specs=(
            P("passage", "dp", None, None),
            P("dp", None, "passage"),
            P("passage"),
            P("passage", None),
        ),
        check_vma=False,
    )
```
